32 devices in a mesh: groups: 2 (over x), blk: 16 (over z, y, core).
Axes of the slice: x: 2, y: 2, z: 4, core: 2. Of those that a mesh axis runs over, the one named last changes fastest.
Arguments:
- tokens: bfloat16 [8192, 8192], P(('groups', 'blk')), parts along dimension 0, may hold values from -6 to 6
- shrink_panels: bfloat16 [32, 8192, 64], P(None, 'blk'), may hold values from -0.0625 to 0.0625
- expand_panels: bfloat16 [32, 64, 8192], P(None, None, 'blk'), may hold values from -0.75 to 0.75
- adapter_scale: float32 [32], replicated, may hold values from 0.5 to 2
- block_adapter: int32 [128, 1], P('groups'), parts along dimension 0, may hold values from 0 to 31
- shard_counts: int32 [32], P('groups'), parts along dimension 0, may hold values from 1 to 256, as said below
Outputs:
- update: bfloat16 [8192, 8192], P(('groups', 'blk')), parts along dimension 0
The draws below stay inside these ranges and needn't reach their ends.
There are 2 independent parts, one for each index of `groups`. The reference program is written for one: setup_inputs(seed, part) draws one part's arguments, and reference() takes and returns one part's arrays. A program takes and returns all parts, laid end to end along the dimension named above; an argument that names none is the same for every part. Nothing has to cross between parts.
Inputs may be any that keep to these rules, and one draw needn't show every extreme that they name: `shard_counts`: every shard holds at least one live row; in every draw some shard is full.
All inputs are finite; a program needn't handle non-finite values.
Results may differ from the reference program's by a relative error of at most 0.0049.
Values may be sent and summed in bfloat16 or wider, within the bound.
No kernel may reach another device: no remote copies, remote signals or barrier semaphores. Data moves between devices by JAX's collectives and lax.ppermute only.
A program may use at most 128 MiB of HBM per device.

```python
import math
import jax
import jax.numpy as jnp
from jax import lax

D = 8192
R = 64
BLOCK = 64
TOK_DEV = 256
TOKENS = 4096
NBLOCKS = 64
ADAPTERS = 32
N_BLK = 16


def draw_shard_counts(key, part):
    values = jax.random.randint(key, (N_BLK,), 1, TOK_DEV + 1, dtype=jnp.int32)
    full_shard = jax.random.randint(jax.random.fold_in(key, 7), (), 0, N_BLK, dtype=jnp.int32)
    marker = jnp.arange(N_BLK, dtype=jnp.int32) == full_shard
    return jnp.where(marker, TOK_DEV, values).astype(jnp.int32)


def steps_of(key, extent, shards, least, largest):
    factor_of, own = 1.0, jax.random.fold_in(key, 6)
    for position, parts in shards:
        draws = jnp.exp(jax.random.uniform(jax.random.fold_in(own, position), (parts,), jnp.float32, least / len(shards), largest / len(shards)))
        factor_of = factor_of * jnp.repeat(draws, extent[position] // parts).reshape([-1 if axis == position else 1 for axis in range(len(extent))])
    return factor_of


def picks_of(key, rows, number_of, top, lift):
    ranking = jax.random.permutation(jax.random.fold_in(key, 1), number_of)
    favour = ranking
    for power in range(3):
        favour = favour * favour // number_of
    favour = favour * lift // number_of
    tickets = jax.random.randint(jax.random.fold_in(key, 2), (rows, number_of), 0, 4096) + favour
    sure = jax.random.permutation(jax.random.fold_in(key, 3), rows)[jnp.arange(number_of) % rows]
    tickets = jnp.where(jnp.arange(rows)[:, None] == sure[None, :], 1 << 14, tickets)
    score = tickets * number_of + jnp.arange(number_of)
    return lax.top_k(score.astype(jnp.int32), top)[1].astype(jnp.int32)


def scatter_about(own_key, shape, spread, bound, split=(), held_as=jnp.bfloat16):
    gain = steps_of(own_key, shape, split, -0.22, 0.18) if split else 1.0
    result = jax.random.normal(own_key, shape, jnp.float32) * spread * gain
    return jnp.minimum(jnp.maximum(result, -bound), bound).astype(held_as)


def setup_inputs(seed: int = 0, part: int = 0) -> dict:
    seeds = jax.random.split(jax.random.key(seed), 7)
    part_keys = jax.random.split(jax.random.fold_in(seeds[6], part), 7)
    tokens = scatter_about(part_keys[0], (TOKENS, D), 1.0, 6.0, ((0, 16),))
    shrink_panels = scatter_about(seeds[1], (ADAPTERS, D, R), D ** -0.5, 0.0625, ((1, 16),))
    expand_panels = scatter_about(seeds[2], (ADAPTERS, R, D), R ** -0.5, 0.75, ((2, 16),))
    adapter_scale = jnp.clip(jnp.exp(jax.random.uniform(seeds[3], (ADAPTERS,), jnp.float32, math.log(0.5), math.log(2.0))), 0.5, 2.0)
    block_adapter = picks_of(part_keys[4], NBLOCKS, ADAPTERS, 1, 512)
    shard_counts = draw_shard_counts(jax.random.fold_in(jax.random.fold_in(seeds[6], part), 71), part)
    return {"tokens": tokens, "shrink_panels": shrink_panels, "expand_panels": expand_panels, "adapter_scale": adapter_scale, "block_adapter": block_adapter, "shard_counts": shard_counts}


def reference(tokens, shrink_panels, expand_panels, adapter_scale, block_adapter, shard_counts):
    block_count = tokens.shape[0] // BLOCK
    blocked = tokens.reshape(block_count, BLOCK, D)
    adapter_ids = block_adapter[:, 0].astype(jnp.int32)

    def one_block(args):
        block_rows, adapter = args
        down_map = lax.dynamic_index_in_dim(shrink_panels, adapter, 0, keepdims=False)
        up_map = lax.dynamic_index_in_dim(expand_panels, adapter, 0, keepdims=False)
        shrunk = jnp.dot(block_rows, down_map, preferred_element_type=jnp.float32).astype(jnp.bfloat16)
        scale_value = lax.dynamic_index_in_dim(adapter_scale, adapter, 0, keepdims=False)
        return jnp.dot(shrunk, up_map, preferred_element_type=jnp.float32) * scale_value

    expanded = lax.map(one_block, (blocked, adapter_ids)).reshape(TOKENS, D)
    within = jnp.arange(TOK_DEV, dtype=jnp.int32)
    live_rows = (within[None, :] < shard_counts[:, None]).reshape(TOKENS, 1)
    return jnp.where(live_rows, expanded, 0.0).astype(jnp.bfloat16)
```

```python
import functools

import jax
import jax.numpy as jnp
from jax import lax
from jax.experimental import pallas as pl
from jax.experimental.pallas import tpu as pltpu
from jax.sharding import PartitionSpec as P

BLOCK = 64


def pack_kernel(ids, panels, out, sem):
    for i in range(out.shape[0]):
        pltpu.make_async_copy(panels.at[ids[i]], out.at[i], sem).start()
    pltpu.make_async_copy(out, out, sem).wait()


def pack(ids, panels):
    count = ids.shape[0]
    return pl.pallas_call(
        pack_kernel,
        out_shape=jax.ShapeDtypeStruct((count, *panels.shape[1:]), panels.dtype),
        in_specs=[pl.BlockSpec(memory_space=pltpu.SMEM), pl.BlockSpec(memory_space=pl.ANY)],
        out_specs=pl.BlockSpec(memory_space=pl.ANY),
        scratch_shapes=[pltpu.SemaphoreType.DMA],
        cost_estimate=pl.CostEstimate(
            flops=0, bytes_accessed=2 * count * panels[0].size * panels.dtype.itemsize, transcendentals=0
        ),
        name="pack",
    )(ids, panels)


def shrink_kernel(tokens, maps, out):
    total = jnp.zeros(out.shape, jnp.float32)
    width = maps.shape[-1]
    for source in range(maps.shape[0]):
        total += lax.dot_general(
            tokens[:, source * width : (source + 1) * width],
            maps[source, 0],
            (((1,), (1,)), ((), ())),
            preferred_element_type=jnp.float32,
        )
    out[...] = total.astype(out.dtype)


def shrink(tokens, maps):
    sources, own, rank, width = maps.shape
    return pl.pallas_call(
        shrink_kernel,
        grid=(own,),
        out_shape=jax.ShapeDtypeStruct((own * BLOCK, rank), tokens.dtype),
        in_specs=[
            pl.BlockSpec((BLOCK, tokens.shape[1]), lambda b: (b, 0)),
            pl.BlockSpec((sources, 1, rank, width), lambda b: (0, b, 0, 0)),
        ],
        out_specs=pl.BlockSpec((BLOCK, rank), lambda b: (b, 0)),
        compiler_params=pltpu.CompilerParams(vmem_limit_bytes=32 * 2**20),
        cost_estimate=pl.CostEstimate(
            flops=2 * tokens.size * rank, bytes_accessed=2 * (tokens.size + maps.size), transcendentals=0
        ),
        name="shrink",
    )(tokens, maps)


def expand_kernel(ids, count, scales, shrunk, maps, out):
    b = pl.program_id(0)
    scale = scales[ids[b]]
    width = maps.shape[-1]
    rows = b * BLOCK + lax.broadcasted_iota(jnp.int32, (BLOCK, width), 0)
    live = rows < count[0]
    for source in range(maps.shape[0]):
        part = jnp.dot(shrunk[...], maps[source, 0], preferred_element_type=jnp.float32)
        out[:, source * width : (source + 1) * width] = jnp.where(live, part * scale, 0.0).astype(out.dtype)


def expand(ids, count, scales, shrunk, maps):
    sources, own, rank, width = maps.shape
    smem = pl.BlockSpec(memory_space=pltpu.SMEM)
    return pl.pallas_call(
        expand_kernel,
        grid=(own,),
        out_shape=jax.ShapeDtypeStruct((own * BLOCK, sources * width), maps.dtype),
        in_specs=[
            smem,
            smem,
            smem,
            pl.BlockSpec((BLOCK, rank), lambda b: (b, 0)),
            pl.BlockSpec((sources, 1, rank, width), lambda b: (0, b, 0, 0)),
        ],
        out_specs=pl.BlockSpec((BLOCK, sources * width), lambda b: (b, 0)),
        compiler_params=pltpu.CompilerParams(vmem_limit_bytes=32 * 2**20),
        cost_estimate=pl.CostEstimate(
            flops=2 * maps.size * BLOCK, bytes_accessed=4 * maps.size, transcendentals=0
        ),
        name="expand",
    )(ids, count, scales, shrunk, maps)


def body(tokens, shrink_panels, expand_panels, adapter_scale, block_adapter, shard_counts):
    devices = shard_counts.shape[0]
    own = tokens.shape[0] // BLOCK
    ids = block_adapter.reshape(-1)
    me = lax.axis_index("blk")
    mine = lax.dynamic_slice_in_dim(ids, me * own, own, 0)
    count = lax.dynamic_slice_in_dim(shard_counts, me, 1, 0)

    def exchange(panels):
        sent = pack(ids, panels)
        got = lax.all_to_all(sent, "blk", split_axis=0, concat_axis=0, tiled=True)
        return got.reshape(devices, own, *panels.shape[1:])

    down = exchange(jnp.swapaxes(shrink_panels, 1, 2))
    up = exchange(expand_panels)
    shrunk = shrink(tokens, down)
    return expand(mine, count, adapter_scale, shrunk, up)


def solution(mesh):
    return jax.shard_map(
        body,
        mesh=mesh,
        in_specs=(
            P(("groups", "blk"), None),
            P(None, "blk", None),
            P(None, None, "blk"),
            P(),
            P("groups", None),
            P("groups"),
        ),
        out_specs=P(("groups", "blk"), None),
        check_vma=False,
    )
```

```python
import functools

import jax
import jax.numpy as jnp
from jax import lax
from jax.experimental import pallas as pl
from jax.experimental.pallas import tpu as pltpu
from jax.sharding import PartitionSpec as P

BLOCK = 64
ROWS = 16
PLANE = 4
VMEM_BYTES = 60 * 2**20

SMEM = pl.BlockSpec(memory_space=pltpu.SMEM)
VMEM = pl.BlockSpec(memory_space=pltpu.VMEM)
HBM = pl.BlockSpec(memory_space=pl.ANY)


SMALL = pl.CostEstimate(flops=0, bytes_accessed=1024, transcendentals=0)


def lists_kernel(dims, caps, where, known, lists, places, pick, slot):
    groups, planes, adapters, stride, own = dims
    plane_blocks = PLANE * own
    blocks = planes * plane_blocks
    row = blocks + planes * PLANE
    my_plane, my_group = where[0], where[1]

    def clear_slot(i, carry):
        slot[i] = -1
        return carry

    def clear_list(i, carry):
        lists[i] = 0
        return carry

    lax.fori_loop(0, planes * adapters, clear_slot, 0)
    lax.fori_loop(0, planes * stride, clear_list, 0)

    def one_plane(plane, largest):
        def one_group(group, found):
            base = lax.rem(my_group - group + groups, groups) * row

            def one_shard(shard, found):
                count = known[base + blocks + plane * PLANE + shard]
                for k in range(own):
                    adapter = known[base + plane * plane_blocks + shard * own + k]
                    at = plane * adapters + adapter
                    held = slot[at]
                    new = jnp.logical_and(count > k * BLOCK, held < 0)
                    slot[at] = jnp.where(new, found, held)
                    lists[plane * stride + found] = jnp.where(new, adapter, 0)
                    found = found + new.astype(jnp.int32)
                return found

            return lax.fori_loop(0, PLANE, one_shard, found)

        return jnp.maximum(largest, lax.fori_loop(0, groups, one_group, 0))

    largest = lax.fori_loop(0, planes, one_plane, 0)
    branch = jnp.int32(0)
    for cap in caps[:-1]:
        branch = branch + (largest > cap).astype(jnp.int32)
    pick[0] = branch

    def one_place(i, carry):
        group, block = i // plane_blocks, lax.rem(i, plane_blocks)
        base = lax.rem(my_group - group + groups, groups) * row
        adapter = known[base + my_plane * plane_blocks + block]
        places[i] = jnp.maximum(slot[my_plane * adapters + adapter], 0)
        return carry

    lax.fori_loop(0, groups * plane_blocks, one_place, 0)


def make_lists(dims, caps, where, known):
    groups, planes, adapters, stride, own = dims
    ints = lambda n: jax.ShapeDtypeStruct((n,), jnp.int32)
    return pl.pallas_call(
        functools.partial(lists_kernel, dims, caps),
        out_shape=(ints(planes * stride), ints(groups * PLANE * own), ints(1)),
        in_specs=[SMEM, SMEM],
        out_specs=(SMEM, SMEM, SMEM),
        scratch_shapes=[pltpu.SMEM((planes * adapters,), jnp.int32)],
        name="lists",
    )(where, known)


def spread_kernel(planes, where, ids, panels, *rest):
    outs, sems = rest[:-1], rest[-1]
    own = outs[0].shape[1]
    for t, out in enumerate(outs):
        shard = lax.rem(where[2] + t, PLANE)

        def send(s, carry, out=out, shard=shard, t=t):
            base = (lax.rem(where[0] + s, planes) * PLANE + shard) * own
            for b in range(own):
                pltpu.make_async_copy(panels.at[ids[base + b]], out.at[s, b], sems.at[t]).start()
            return carry

        lax.fori_loop(0, planes, send, 0)
    for t, out in enumerate(outs):
        pltpu.make_async_copy(out, out, sems.at[t]).wait()


def spread(dims, where, ids, panels):
    groups, planes, adapters, stride, own = dims
    out = jax.ShapeDtypeStruct((planes, own, *panels.shape[1:]), panels.dtype)
    return pl.pallas_call(
        functools.partial(spread_kernel, planes),
        out_shape=(out,) * PLANE,
        in_specs=[SMEM, SMEM, VMEM],
        out_specs=(HBM,) * PLANE,
        scratch_shapes=[pltpu.SemaphoreType.DMA((PLANE,))],
        compiler_params=pltpu.CompilerParams(vmem_limit_bytes=VMEM_BYTES),
        cost_estimate=SMALL,
        name="spread",
    )(where, ids, panels)


def regroup_kernel(planes, where, *refs):
    held, out, sem = refs[:PLANE], refs[PLANE], refs[-1]
    for s in range(planes):
        plane = lax.rem(where[0] + s, planes)
        for t in range(PLANE):
            pltpu.make_async_copy(held[t].at[s], out.at[plane, t], sem).start()
    pltpu.make_async_copy(out, out, sem).wait()


def regroup(where, held):
    planes = held[0].shape[0]
    return pl.pallas_call(
        functools.partial(regroup_kernel, planes),
        out_shape=jax.ShapeDtypeStruct((planes, PLANE, *held[0].shape[1:]), held[0].dtype),
        in_specs=[SMEM, *[VMEM] * PLANE],
        out_specs=HBM,
        scratch_shapes=[pltpu.SemaphoreType.DMA],
        compiler_params=pltpu.CompilerParams(vmem_limit_bytes=VMEM_BYTES),
        cost_estimate=SMALL,
        name="regroup",
    )(where, *held)


def plane_pack_kernel(planes, stride, first, where, lists, panels, *rest):
    outs, sems = rest[:-1], rest[-1]
    ranks = outs[0].shape[1]
    mine = pl.ds(pl.multiple_of(first + where[1] * ranks, ranks), ranks)
    for i, out in enumerate(outs):
        base = lax.rem(where[0] + i + 1, planes) * stride

        def send(k, carry, out=out, base=base, i=i):
            pltpu.make_async_copy(panels.at[lists[base + k], mine], out.at[k], sems.at[i]).start()
            return carry

        lax.fori_loop(0, out.shape[0], send, 0)
    for i, out in enumerate(outs):
        pltpu.make_async_copy(out, out, sems.at[i]).wait()


def plane_pack(dims, cap, first, ranks, where, lists, panels):
    groups, planes, adapters, stride, own = dims
    out = jax.ShapeDtypeStruct((cap, ranks // groups, panels.shape[2]), panels.dtype)
    return pl.pallas_call(
        functools.partial(plane_pack_kernel, planes, stride, first),
        out_shape=(out,) * (planes - 1),
        in_specs=[SMEM, SMEM, VMEM],
        out_specs=(HBM,) * (planes - 1),
        scratch_shapes=[pltpu.SemaphoreType.DMA((planes - 1,))],
        compiler_params=pltpu.CompilerParams(vmem_limit_bytes=VMEM_BYTES),
        cost_estimate=SMALL,
        name="plane_pack",
    )(where, lists, panels)


def group_pack_kernel(groups, planes, where, places, *rest):
    got, outs, sems = rest[: planes - 1], rest[planes - 1 : -1], rest[-1]
    blocks = outs[0].shape[0]
    for i, out in enumerate(outs):
        base = lax.rem(where[1] + i + 1, groups) * blocks

        def send(j, carry, out=out, base=base, i=i):
            place = places[base + j]
            for s in range(planes - 1):
                pltpu.make_async_copy(got[s].at[place], out.at[j, s], sems.at[i]).start()
            return carry

        lax.fori_loop(0, blocks, send, 0)
    for i, out in enumerate(outs):
        pltpu.make_async_copy(out, out, sems.at[i]).wait()


def group_pack(dims, where, places, got):
    groups, planes, adapters, stride, own = dims
    out = jax.ShapeDtypeStruct((PLANE * own, planes - 1, *got[0].shape[1:]), got[0].dtype)
    return pl.pallas_call(
        functools.partial(group_pack_kernel, groups, planes),
        out_shape=(out,) * (groups - 1),
        in_specs=[SMEM, SMEM, *[VMEM] * (planes - 1)],
        out_specs=(HBM,) * (groups - 1),
        scratch_shapes=[pltpu.SemaphoreType.DMA((groups - 1,))],
        compiler_params=pltpu.CompilerParams(vmem_limit_bytes=VMEM_BYTES),
        cost_estimate=SMALL,
        name="group_pack",
    )(where, places, *got)


def shard_pack_kernel(groups, planes, first, where, places, ids, panels, *rest):
    got = rest[: planes - 1]
    swapped = rest[planes - 1 : planes + groups - 2]
    outs, sems = rest[planes + groups - 2 : -1], rest[-1]
    own = outs[0].shape[0]
    ranks = got[0].shape[1]
    my_group, my_shard = where[1], where[2]

    def part(group):
        return pl.ds(pl.multiple_of(group * ranks, ranks), ranks)

    for t, out in enumerate(outs):
        shard = lax.rem(my_shard + t, PLANE)

        def send(b, carry, out=out, shard=shard, t=t):
            j = shard * own + b
            place = places[my_group * PLANE * own + j]
            copy = lambda src, dst: pltpu.make_async_copy(src, dst, sems.at[t]).start()
            copy(panels.at[ids[j], pl.ds(first, out.shape[2])], out.at[b, 0])
            for s in range(planes - 1):
                copy(got[s].at[place], out.at[b, s + 1, part(my_group)])
            for d in range(groups - 1):
                other = lax.rem(my_group + groups - d - 1, groups)
                copy(swapped[d].at[j], out.at[b, pl.ds(1, planes - 1), part(other)])
            return carry

        lax.fori_loop(0, own, send, 0)
    for t, out in enumerate(outs):
        pltpu.make_async_copy(out, out, sems.at[t]).wait()


def shard_pack(dims, first, ranks, where, places, ids, panels, got, swapped):
    groups, planes, adapters, stride, own = dims
    out = jax.ShapeDtypeStruct((own, planes, ranks, panels.shape[2]), panels.dtype)
    return pl.pallas_call(
        functools.partial(shard_pack_kernel, groups, planes, first),
        out_shape=(out,) * PLANE,
        in_specs=[SMEM, SMEM, SMEM, VMEM, *[VMEM] * (planes + groups - 2)],
        out_specs=(HBM,) * PLANE,
        scratch_shapes=[pltpu.SemaphoreType.DMA((PLANE,))],
        compiler_params=pltpu.CompilerParams(vmem_limit_bytes=VMEM_BYTES),
        cost_estimate=SMALL,
        name="shard_pack",
    )(where, places, ids, panels, *got, *swapped)


def shrink_kernel(planes, where, tokens, *rest):
    maps, out = rest[:-1], rest[-1]
    width = maps[0].shape[-1]
    total = jnp.zeros(out.shape, jnp.float32)
    for t in range(PLANE):
        shard = lax.rem(where[2] + PLANE - t, PLANE)
        for s in range(planes):
            source = lax.rem(where[0] + planes - s, planes) * PLANE + shard
            total += lax.dot_general(
                tokens[:, pl.ds(pl.multiple_of(source * width, width), width)],
                jnp.concatenate([m[0, s] for m in maps[t::PLANE]], axis=0),
                (((1,), (1,)), ((), ())),
                preferred_element_type=jnp.float32,
            )
    out[...] = total.astype(out.dtype)


def shrink(where, tokens, maps):
    own, planes, ranks, width = maps[0].shape
    rank = len(maps) // PLANE * ranks
    return pl.pallas_call(
        functools.partial(shrink_kernel, planes),
        grid=(own,),
        out_shape=jax.ShapeDtypeStruct((own * BLOCK, rank), tokens.dtype),
        in_specs=[
            SMEM,
            pl.BlockSpec((BLOCK, tokens.shape[1]), lambda b: (b, 0)),
            *[pl.BlockSpec((1, planes, ranks, width), lambda b: (b, 0, 0, 0))] * len(maps),
        ],
        out_specs=pl.BlockSpec((BLOCK, rank), lambda b: (b, 0)),
        compiler_params=pltpu.CompilerParams(vmem_limit_bytes=VMEM_BYTES),
        cost_estimate=SMALL,
        name="shrink",
    )(where, tokens, *maps)


def expand_kernel(planes, where, ids, count, scales, shrunk, maps, out):
    b = pl.program_id(0)
    scale = scales[ids[b]]
    width = maps.shape[-1]
    rows = b * BLOCK + lax.broadcasted_iota(jnp.int32, (BLOCK, width), 0)
    live = rows < count[0]
    for plane in range(planes):
        for t in range(PLANE):
            source = plane * PLANE + lax.rem(where[2] + PLANE - t, PLANE)
            part = jnp.dot(shrunk[...], maps[plane, t, 0], preferred_element_type=jnp.float32)
            columns = pl.ds(pl.multiple_of(source * width, width), width)
            out[:, columns] = jnp.where(live, part * scale, 0.0).astype(out.dtype)


def expand(where, ids, count, scales, shrunk, maps):
    planes, _, own, rank, width = maps.shape
    columns = planes * PLANE * width
    return pl.pallas_call(
        functools.partial(expand_kernel, planes),
        grid=(own,),
        out_shape=jax.ShapeDtypeStruct((own * BLOCK, columns), shrunk.dtype),
        in_specs=[
            *[SMEM] * 4,
            pl.BlockSpec((BLOCK, rank), lambda b: (b, 0)),
            pl.BlockSpec((planes, PLANE, 1, rank, width), lambda b: (0, 0, b, 0, 0)),
        ],
        out_specs=pl.BlockSpec((BLOCK, columns), lambda b: (b, 0)),
        compiler_params=pltpu.CompilerParams(vmem_limit_bytes=VMEM_BYTES),
        cost_estimate=SMALL,
        name="expand",
    )(where, ids, count, scales, shrunk, maps)


def body(groups, tokens, shrink_panels, expand_panels, adapter_scale, block_adapter, shard_counts):
    devices = shard_counts.shape[0]
    own = tokens.shape[0] // BLOCK
    planes = devices // PLANE
    adapters = shrink_panels.shape[0]
    most = min(adapters, groups * PLANE * own)
    dims = (groups, planes, adapters, most + 1, own)
    caps = tuple(most * part // 16 for part in (8, 9, 10, 11, 13, 16))

    ids = block_adapter.reshape(-1)
    me, group = lax.axis_index("blk"), lax.axis_index("groups")
    where = jnp.stack([me // PLANE, group, lax.rem(me, PLANE)]).astype(jnp.int32)
    facts = jnp.concatenate([ids, shard_counts])
    known = [facts]
    for d in range(1, groups):
        known.append(lax.ppermute(facts, "groups", [(i, (i + d) % groups) for i in range(groups)]))
    lists, places, pick = make_lists(dims, caps, where, jnp.concatenate(known))
    plane_ids = lax.dynamic_slice_in_dim(ids, me // PLANE * PLANE * own, PLANE * own, 0)
    mine = lax.dynamic_slice_in_dim(ids, me * own, own, 0)
    count = lax.dynamic_slice_in_dim(shard_counts, me, 1, 0)
    down_panels = jnp.swapaxes(shrink_panels, 1, 2)

    def plane_shift(x, s):
        return lax.ppermute(x, "blk", [(i, (i + s * PLANE) % devices) for i in range(devices)])

    def group_shift(x, d):
        return lax.ppermute(x, "groups", [(i, (i + d) % groups) for i in range(groups)])

    def shard_shift(x, t):
        pairs = [(i, i // PLANE * PLANE + (i + t) % PLANE) for i in range(devices)]
        return lax.ppermute(x, "blk", pairs)

    rank = expand_panels.shape[1]
    parts = 2 if rank % (2 * groups * ROWS) == 0 else 1
    ranks = rank // parts

    up_sent = spread(dims, where, ids, expand_panels)

    def run(cap):
        def branch(up_sent):
            sent = [plane_pack(dims, cap, h * ranks, ranks, where, lists, down_panels) for h in range(parts)]
            near = [up_sent[0], *[shard_shift(up_sent[t], t) for t in range(1, PLANE)]]
            up_packed = regroup(where, near)
            got, maps = [], []
            for h in range(parts):
                got.append([plane_shift(x, s + 1) for s, x in enumerate(sent[h])])
                if h + 1 < parts:
                    got[h], sent[h + 1] = lax.optimization_barrier((got[h], sent[h + 1]))
                else:
                    got[h], up_packed = lax.optimization_barrier((got[h], up_packed))
                swaps = group_pack(dims, where, places, got[h])
                swapped = [group_shift(x, d + 1) for d, x in enumerate(swaps)]
                maps.append(
                    shard_pack(dims, h * ranks, ranks, where, places, plane_ids, down_panels, got[h], swapped)
                )
            mirrors = [list(range(i, devices, PLANE)) for i in range(PLANE)]
            up = lax.all_to_all(up_packed, "blk", split_axis=0, concat_axis=0, tiled=True, axis_index_groups=mirrors)
            down = []
            for kept, *moved in maps:
                down += [kept, *[shard_shift(x, t + 1) for t, x in enumerate(moved)]]
            shrunk = shrink(where, tokens, down)
            return expand(where, mine, count, adapter_scale, shrunk, up)

        return branch

    return lax.switch(pick[0], [run(cap) for cap in caps], up_sent)


def solution(mesh):
    return jax.shard_map(
        functools.partial(body, mesh.shape["groups"]),
        mesh=mesh,
        in_specs=(
            P(("groups", "blk"), None),
            P(None, "blk", None),
            P(None, None, "blk"),
            P(),
            P("groups", None),
            P("groups"),
        ),
        out_specs=P(("groups", "blk"), None),
        check_vma=False,
    )
```

```python
import functools

import jax
import jax.numpy as jnp
from jax import lax
from jax.experimental import pallas as pl
from jax.experimental.pallas import tpu as pltpu
from jax.sharding import PartitionSpec as P

BLOCK = 64
ROWS = 16
PLANE = 4
VMEM_BYTES = 60 * 2**20

SMEM = pl.BlockSpec(memory_space=pltpu.SMEM)
VMEM = pl.BlockSpec(memory_space=pltpu.VMEM)
HBM = pl.BlockSpec(memory_space=pl.ANY)


SMALL = pl.CostEstimate(flops=0, bytes_accessed=1024, transcendentals=0)


def prepare_kernel(dims, caps, where, *rest):
    groups, planes, adapters, stride, own = dims
    facts, panels = rest[:groups], rest[groups]
    sent, (lists, places, pick, slot, known, sems) = rest[groups + 1 : groups + 1 + PLANE], rest[groups + 1 + PLANE :]
    plane_blocks = PLANE * own
    blocks = planes * plane_blocks
    row = blocks + planes * PLANE
    my_plane, my_group, my_shard = where[0], where[1], where[2]

    for t, out in enumerate(sent):
        shard = lax.rem(my_shard + t, PLANE)

        def send(s, carry, out=out, shard=shard, t=t):
            base = (lax.rem(my_plane + s, planes) * PLANE + shard) * own
            for b in range(own):
                pltpu.make_async_copy(panels.at[facts[0][base + b]], out.at[s, b], sems.at[t]).start()
            return carry

        lax.fori_loop(0, planes, send, 0)

    for d, fact in enumerate(facts):
        base = lax.rem(my_group - d + groups, groups) * row

        def keep(i, carry, fact=fact, base=base):
            for k in range(PLANE):
                known[base + i * PLANE + k] = fact[i * PLANE + k]
            return carry

        lax.fori_loop(0, row // PLANE, keep, 0)

    def one_plane(plane, largest):
        at_slot, at_list = plane * adapters, plane * stride

        def clear(i, carry):
            for k in range(8):
                slot[at_slot + i * 8 + k] = -1
            return carry

        lax.fori_loop(0, adapters // 8, clear, 0)
        found = jnp.int32(0)
        for group in range(groups):
            for shard in range(PLANE):
                count = known[group * row + blocks + plane * PLANE + shard]
                for k in range(own):
                    adapter = known[group * row + plane * plane_blocks + shard * own + k]
                    held = slot[at_slot + adapter]
                    new = jnp.logical_and(count > k * BLOCK, held < 0)
                    slot[at_slot + adapter] = jnp.where(new, found, held)
                    lists[at_list + found] = adapter
                    found = found + new.astype(jnp.int32)

        def fill(i, carry):
            lists[at_list + i] = 0
            return carry

        lax.fori_loop(found, stride, fill, 0)
        return jnp.maximum(largest, found)

    largest = lax.fori_loop(0, planes, one_plane, jnp.int32(0))
    branch = jnp.int32(0)
    for cap in caps[:-1]:
        branch = branch + (largest > cap).astype(jnp.int32)
    pick[0] = branch

    def one_group(group, carry):
        for block in range(plane_blocks):
            adapter = known[group * row + my_plane * plane_blocks + block]
            places[group * plane_blocks + block] = jnp.maximum(slot[my_plane * adapters + adapter], 0)
        return carry

    lax.fori_loop(0, groups, one_group, 0)
    for t, out in enumerate(sent):
        pltpu.make_async_copy(out, out, sems.at[t]).wait()


def prepare(dims, caps, where, facts, panels):
    groups, planes, adapters, stride, own = dims
    ints = lambda n: jax.ShapeDtypeStruct((n,), jnp.int32)
    sent = jax.ShapeDtypeStruct((planes, own, *panels.shape[1:]), panels.dtype)
    row = planes * PLANE * (own + 1)
    return pl.pallas_call(
        functools.partial(prepare_kernel, dims, caps),
        out_shape=(*(sent,) * PLANE, ints(planes * stride), ints(groups * PLANE * own), ints(1)),
        in_specs=[SMEM, *[SMEM] * groups, VMEM],
        out_specs=(*(HBM,) * PLANE, SMEM, SMEM, SMEM),
        scratch_shapes=[
            pltpu.SMEM((planes * adapters,), jnp.int32),
            pltpu.SMEM((groups * row,), jnp.int32),
            pltpu.SemaphoreType.DMA((PLANE,)),
        ],
        compiler_params=pltpu.CompilerParams(vmem_limit_bytes=VMEM_BYTES),
        cost_estimate=SMALL,
        name="prepare",
    )(where, *facts, panels)


def regroup_kernel(planes, where, *refs):
    held, out, sem = refs[:PLANE], refs[PLANE], refs[-1]
    for s in range(planes):
        plane = lax.rem(where[0] + s, planes)
        for t in range(PLANE):
            pltpu.make_async_copy(held[t].at[s], out.at[plane, t], sem).start()
    pltpu.make_async_copy(out, out, sem).wait()


def regroup(where, held):
    planes = held[0].shape[0]
    return pl.pallas_call(
        functools.partial(regroup_kernel, planes),
        out_shape=jax.ShapeDtypeStruct((planes, PLANE, *held[0].shape[1:]), held[0].dtype),
        in_specs=[SMEM, *[VMEM] * PLANE],
        out_specs=HBM,
        scratch_shapes=[pltpu.SemaphoreType.DMA],
        compiler_params=pltpu.CompilerParams(vmem_limit_bytes=VMEM_BYTES),
        cost_estimate=SMALL,
        name="regroup",
    )(where, *held)


def plane_pack_kernel(planes, stride, first, where, lists, panels, *rest):
    outs, sems = rest[:-1], rest[-1]
    ranks = outs[0].shape[1]
    mine = pl.ds(pl.multiple_of(first + where[1] * ranks, ranks), ranks)
    for i, out in enumerate(outs):
        base = lax.rem(where[0] + i + 1, planes) * stride

        def send(k, carry, out=out, base=base, i=i):
            pltpu.make_async_copy(panels.at[lists[base + k], mine], out.at[k], sems.at[i]).start()
            return carry

        lax.fori_loop(0, out.shape[0], send, 0)
    for i, out in enumerate(outs):
        pltpu.make_async_copy(out, out, sems.at[i]).wait()


def plane_pack(dims, cap, first, ranks, where, lists, panels):
    groups, planes, adapters, stride, own = dims
    out = jax.ShapeDtypeStruct((cap, ranks // groups, panels.shape[2]), panels.dtype)
    return pl.pallas_call(
        functools.partial(plane_pack_kernel, planes, stride, first),
        out_shape=(out,) * (planes - 1),
        in_specs=[SMEM, SMEM, VMEM],
        out_specs=(HBM,) * (planes - 1),
        scratch_shapes=[pltpu.SemaphoreType.DMA((planes - 1,))],
        compiler_params=pltpu.CompilerParams(vmem_limit_bytes=VMEM_BYTES),
        cost_estimate=SMALL,
        name="plane_pack",
    )(where, lists, panels)


def group_pack_kernel(groups, planes, where, places, *rest):
    got, outs, sems = rest[: planes - 1], rest[planes - 1 : -1], rest[-1]
    blocks = outs[0].shape[0]
    for i, out in enumerate(outs):
        base = lax.rem(where[1] + i + 1, groups) * blocks

        def send(j, carry, out=out, base=base, i=i):
            place = places[base + j]
            for s in range(planes - 1):
                pltpu.make_async_copy(got[s].at[place], out.at[j, s], sems.at[i]).start()
            return carry

        lax.fori_loop(0, blocks, send, 0)
    for i, out in enumerate(outs):
        pltpu.make_async_copy(out, out, sems.at[i]).wait()


def group_pack(dims, where, places, got):
    groups, planes, adapters, stride, own = dims
    out = jax.ShapeDtypeStruct((PLANE * own, planes - 1, *got[0].shape[1:]), got[0].dtype)
    return pl.pallas_call(
        functools.partial(group_pack_kernel, groups, planes),
        out_shape=(out,) * (groups - 1),
        in_specs=[SMEM, SMEM, *[VMEM] * (planes - 1)],
        out_specs=(HBM,) * (groups - 1),
        scratch_shapes=[pltpu.SemaphoreType.DMA((groups - 1,))],
        compiler_params=pltpu.CompilerParams(vmem_limit_bytes=VMEM_BYTES),
        cost_estimate=SMALL,
        name="group_pack",
    )(where, places, *got)


def shard_pack_kernel(groups, planes, first, where, places, ids, panels, *rest):
    got = rest[: planes - 1]
    swapped = rest[planes - 1 : planes + groups - 2]
    outs, sems = rest[planes + groups - 2 : -1], rest[-1]
    own = outs[0].shape[0]
    ranks = got[0].shape[1]
    my_group, my_shard = where[1], where[2]

    def part(group):
        return pl.ds(pl.multiple_of(group * ranks, ranks), ranks)

    for t, out in enumerate(outs):
        shard = lax.rem(my_shard + t, PLANE)

        def send(b, carry, out=out, shard=shard, t=t):
            j = shard * own + b
            place = places[my_group * PLANE * own + j]
            copy = lambda src, dst: pltpu.make_async_copy(src, dst, sems.at[t]).start()
            copy(panels.at[ids[j], pl.ds(first, out.shape[2])], out.at[b, 0])
            for s in range(planes - 1):
                copy(got[s].at[place], out.at[b, s + 1, part(my_group)])
            for d in range(groups - 1):
                other = lax.rem(my_group + groups - d - 1, groups)
                copy(swapped[d].at[j], out.at[b, pl.ds(1, planes - 1), part(other)])
            return carry

        lax.fori_loop(0, own, send, 0)
    for t, out in enumerate(outs):
        pltpu.make_async_copy(out, out, sems.at[t]).wait()


def shard_pack(dims, first, ranks, where, places, ids, panels, got, swapped):
    groups, planes, adapters, stride, own = dims
    out = jax.ShapeDtypeStruct((own, planes, ranks, panels.shape[2]), panels.dtype)
    return pl.pallas_call(
        functools.partial(shard_pack_kernel, groups, planes, first),
        out_shape=(out,) * PLANE,
        in_specs=[SMEM, SMEM, SMEM, VMEM, *[VMEM] * (planes + groups - 2)],
        out_specs=(HBM,) * PLANE,
        scratch_shapes=[pltpu.SemaphoreType.DMA((PLANE,))],
        compiler_params=pltpu.CompilerParams(vmem_limit_bytes=VMEM_BYTES),
        cost_estimate=SMALL,
        name="shard_pack",
    )(where, places, ids, panels, *got, *swapped)


def shrink_kernel(planes, where, tokens, *rest):
    maps, out = rest[:-1], rest[-1]
    width = maps[0].shape[-1]
    total = jnp.zeros(out.shape, jnp.float32)
    for t in range(PLANE):
        shard = lax.rem(where[2] + PLANE - t, PLANE)
        for s in range(planes):
            source = lax.rem(where[0] + planes - s, planes) * PLANE + shard
            total += lax.dot_general(
                tokens[:, pl.ds(pl.multiple_of(source * width, width), width)],
                jnp.concatenate([m[0, s] for m in maps[t::PLANE]], axis=0),
                (((1,), (1,)), ((), ())),
                preferred_element_type=jnp.float32,
            )
    out[...] = total.astype(out.dtype)


def shrink(where, tokens, maps):
    own, planes, ranks, width = maps[0].shape
    rank = len(maps) // PLANE * ranks
    return pl.pallas_call(
        functools.partial(shrink_kernel, planes),
        grid=(own,),
        out_shape=jax.ShapeDtypeStruct((own * BLOCK, rank), tokens.dtype),
        in_specs=[
            SMEM,
            pl.BlockSpec((BLOCK, tokens.shape[1]), lambda b: (b, 0)),
            *[pl.BlockSpec((1, planes, ranks, width), lambda b: (b, 0, 0, 0))] * len(maps),
        ],
        out_specs=pl.BlockSpec((BLOCK, rank), lambda b: (b, 0)),
        compiler_params=pltpu.CompilerParams(vmem_limit_bytes=VMEM_BYTES),
        cost_estimate=SMALL,
        name="shrink",
    )(where, tokens, *maps)


def expand_kernel(planes, where, ids, count, scales, shrunk, maps, out):
    b = pl.program_id(0)
    scale = scales[ids[b]]
    width = maps.shape[-1]
    rows = b * BLOCK + lax.broadcasted_iota(jnp.int32, (BLOCK, width), 0)
    live = rows < count[0]
    for plane in range(planes):
        for t in range(PLANE):
            source = plane * PLANE + lax.rem(where[2] + PLANE - t, PLANE)
            part = jnp.dot(shrunk[...], maps[plane, t, 0], preferred_element_type=jnp.float32)
            columns = pl.ds(pl.multiple_of(source * width, width), width)
            out[:, columns] = jnp.where(live, part * scale, 0.0).astype(out.dtype)


def expand(where, ids, count, scales, shrunk, maps):
    planes, _, own, rank, width = maps.shape
    columns = planes * PLANE * width
    return pl.pallas_call(
        functools.partial(expand_kernel, planes),
        grid=(own,),
        out_shape=jax.ShapeDtypeStruct((own * BLOCK, columns), shrunk.dtype),
        in_specs=[
            *[SMEM] * 4,
            pl.BlockSpec((BLOCK, rank), lambda b: (b, 0)),
            pl.BlockSpec((planes, PLANE, 1, rank, width), lambda b: (0, 0, b, 0, 0)),
        ],
        out_specs=pl.BlockSpec((BLOCK, columns), lambda b: (b, 0)),
        compiler_params=pltpu.CompilerParams(vmem_limit_bytes=VMEM_BYTES),
        cost_estimate=SMALL,
        name="expand",
    )(where, ids, count, scales, shrunk, maps)


def body(groups, tokens, shrink_panels, expand_panels, adapter_scale, block_adapter, shard_counts):
    devices = shard_counts.shape[0]
    own = tokens.shape[0] // BLOCK
    planes = devices // PLANE
    adapters = shrink_panels.shape[0]
    most = min(adapters, groups * PLANE * own)
    dims = (groups, planes, adapters, most + 1, own)
    caps = tuple(most * part // 32 for part in (15, 16, 17, 18, 19, 20, 21, 23, 26, 32))

    ids = block_adapter.reshape(-1)
    me, group = lax.axis_index("blk"), lax.axis_index("groups")
    where = jnp.stack([me // PLANE, group, lax.rem(me, PLANE)]).astype(jnp.int32)
    facts = jnp.concatenate([ids, shard_counts])
    known = [facts]
    for d in range(1, groups):
        known.append(lax.ppermute(facts, "groups", [(i, (i + d) % groups) for i in range(groups)]))
    *up_sent, lists, places, pick = prepare(dims, caps, where, known, expand_panels)
    plane_ids = lax.dynamic_slice_in_dim(ids, me // PLANE * PLANE * own, PLANE * own, 0)
    mine = lax.dynamic_slice_in_dim(ids, me * own, own, 0)
    count = lax.dynamic_slice_in_dim(shard_counts, me, 1, 0)
    down_panels = jnp.swapaxes(shrink_panels, 1, 2)

    def plane_shift(x, s):
        return lax.ppermute(x, "blk", [(i, (i + s * PLANE) % devices) for i in range(devices)])

    def group_shift(x, d):
        return lax.ppermute(x, "groups", [(i, (i + d) % groups) for i in range(groups)])

    def shard_shift(x, t):
        pairs = [(i, i // PLANE * PLANE + (i + t) % PLANE) for i in range(devices)]
        return lax.ppermute(x, "blk", pairs)

    rank = expand_panels.shape[1]
    parts = 2 if rank % (2 * groups * ROWS) == 0 else 1
    ranks = rank // parts


    def run(cap):
        def branch(up_sent):
            sent = [plane_pack(dims, cap, h * ranks, ranks, where, lists, down_panels) for h in range(parts)]
            near = [up_sent[0], *[shard_shift(up_sent[t], t) for t in range(1, PLANE)]]
            up_packed = regroup(where, near)
            got, maps = [], []
            for h in range(parts):
                got.append([plane_shift(x, s + 1) for s, x in enumerate(sent[h])])
                if h + 1 < parts:
                    got[h], sent[h + 1] = lax.optimization_barrier((got[h], sent[h + 1]))
                else:
                    got[h], up_packed = lax.optimization_barrier((got[h], up_packed))
                swaps = group_pack(dims, where, places, got[h])
                swapped = [group_shift(x, d + 1) for d, x in enumerate(swaps)]
                maps.append(
                    shard_pack(dims, h * ranks, ranks, where, places, plane_ids, down_panels, got[h], swapped)
                )
            mirrors = [list(range(i, devices, PLANE)) for i in range(PLANE)]
            up = lax.all_to_all(up_packed, "blk", split_axis=0, concat_axis=0, tiled=True, axis_index_groups=mirrors)
            down = []
            for kept, *moved in maps:
                down += [kept, *[shard_shift(x, t + 1) for t, x in enumerate(moved)]]
            shrunk = shrink(where, tokens, down)
            return expand(where, mine, count, adapter_scale, shrunk, up)

        return branch

    return lax.switch(pick[0], [run(cap) for cap in caps], up_sent)


def solution(mesh):
    return jax.shard_map(
        functools.partial(body, mesh.shape["groups"]),
        mesh=mesh,
        in_specs=(
            P(("groups", "blk"), None),
            P(None, "blk", None),
            P(None, None, "blk"),
            P(),
            P("groups", None),
            P("groups"),
        ),
        out_specs=P(("groups", "blk"), None),
        check_vma=False,
    )
```

```python
import functools

import jax
import jax.numpy as jnp
from jax import lax
from jax.experimental import pallas as pl
from jax.experimental.pallas import tpu as pltpu
from jax.sharding import PartitionSpec as P

BLOCK = 64
ROWS = 16
CAPS = ((16, 4), (17, 4), (18, 4), (18, 5), (19, 5), (20, 5), (21, 6), (24, 6), (32, 8))
PLANE = 4
VMEM_BYTES = 60 * 2**20

SMEM = pl.BlockSpec(memory_space=pltpu.SMEM)
VMEM = pl.BlockSpec(memory_space=pltpu.VMEM)
HBM = pl.BlockSpec(memory_space=pl.ANY)


SMALL = pl.CostEstimate(flops=0, bytes_accessed=1024, transcendentals=0)


def prepare_kernel(dims, caps, where, *rest):
    groups, planes, adapters, stride, last_stride, own = dims
    facts, panels = rest[:groups], rest[groups]
    sent, rest = rest[groups + 1 : groups + 1 + PLANE], rest[groups + 1 + PLANE :]
    lists, last_lists, places, last_places, pick, slot, last_slot, known, sems = rest
    plane_blocks = PLANE * own
    blocks = planes * plane_blocks
    row = blocks + planes * PLANE
    my_plane, my_group, my_shard = where[0], where[1], where[2]

    for t, out in enumerate(sent):
        shard = lax.rem(my_shard + t, PLANE)

        def send(s, carry, out=out, shard=shard, t=t):
            base = (lax.rem(my_plane + s, planes) * PLANE + shard) * own
            for b in range(own - 1):
                pltpu.make_async_copy(panels.at[facts[0][base + b]], out.at[s, b], sems.at[t]).start()
            return carry

        lax.fori_loop(0, planes, send, 0)

    for d, fact in enumerate(facts):
        base = lax.rem(my_group - d + groups, groups) * row

        def keep(i, carry, fact=fact, base=base):
            for k in range(PLANE):
                known[base + i * PLANE + k] = fact[i * PLANE + k]
            return carry

        lax.fori_loop(0, row // PLANE, keep, 0)

    def one_plane(plane, largest):
        at_slot, at_list, at_last = plane * adapters, plane * stride, plane * last_stride

        def clear(i, carry):
            for k in range(8):
                slot[at_slot + i * 8 + k] = -1
                last_slot[at_slot + i * 8 + k] = -1
            return carry

        lax.fori_loop(0, adapters // 8, clear, 0)
        found, last_found = jnp.int32(0), jnp.int32(0)
        for group in range(groups):
            for shard in range(PLANE):
                count = known[group * row + blocks + plane * PLANE + shard]
                for k in range(own):
                    adapter = known[group * row + plane * plane_blocks + shard * own + k]
                    held = slot[at_slot + adapter]
                    new = jnp.logical_and(count > k * BLOCK, held < 0)
                    slot[at_slot + adapter] = jnp.where(new, found, held)
                    lists[at_list + found] = adapter
                    found = found + new.astype(jnp.int32)
                held = last_slot[at_slot + adapter]
                new = jnp.logical_and(count > (own - 1) * BLOCK, held < 0)
                last_slot[at_slot + adapter] = jnp.where(new, last_found, held)
                last_lists[at_last + last_found] = adapter
                last_found = last_found + new.astype(jnp.int32)

        def fill(i, carry):
            lists[at_list + i] = 0
            return carry

        def fill_last(i, carry):
            last_lists[at_last + i] = 0
            return carry

        lax.fori_loop(found, stride, fill, 0)
        lax.fori_loop(last_found, last_stride, fill_last, 0)
        return jnp.maximum(largest[0], found), jnp.maximum(largest[1], last_found)

    largest, last_largest = lax.fori_loop(0, planes, one_plane, (jnp.int32(0), jnp.int32(0)))
    branch = jnp.int32(0)
    for cap, last_cap in caps[:-1]:
        branch = branch + jnp.logical_or(largest > cap, last_largest > last_cap).astype(jnp.int32)
    pick[0] = branch

    def one_group(group, carry):
        for block in range(plane_blocks):
            adapter = known[group * row + my_plane * plane_blocks + block]
            places[group * plane_blocks + block] = jnp.maximum(slot[my_plane * adapters + adapter], 0)
            if block % own == own - 1:
                place = jnp.maximum(last_slot[my_plane * adapters + adapter], 0)
                last_places[group * PLANE + block // own] = place
        return carry

    lax.fori_loop(0, groups, one_group, 0)
    for t, out in enumerate(sent):
        pltpu.make_async_copy(out, out, sems.at[t]).wait()


def prepare(dims, caps, where, facts, panels):
    groups, planes, adapters, stride, last_stride, own = dims
    ints = lambda n: jax.ShapeDtypeStruct((n,), jnp.int32)
    sent = jax.ShapeDtypeStruct((planes, own - 1, *panels.shape[1:]), panels.dtype)
    row = planes * PLANE * (own + 1)
    counts = (planes * stride, planes * last_stride, groups * PLANE * own, groups * PLANE, 1)
    return pl.pallas_call(
        functools.partial(prepare_kernel, dims, caps),
        out_shape=(*(sent,) * PLANE, *map(ints, counts)),
        in_specs=[SMEM, *[SMEM] * groups, VMEM],
        out_specs=(*(HBM,) * PLANE, *(SMEM,) * len(counts)),
        scratch_shapes=[
            pltpu.SMEM((planes * adapters,), jnp.int32),
            pltpu.SMEM((planes * adapters,), jnp.int32),
            pltpu.SMEM((groups * row,), jnp.int32),
            pltpu.SemaphoreType.DMA((PLANE,)),
        ],
        compiler_params=pltpu.CompilerParams(vmem_limit_bytes=VMEM_BYTES),
        cost_estimate=SMALL,
        name="prepare",
    )(where, *facts, panels)


def regroup_kernel(planes, where, *refs):
    held, out, sem = refs[:PLANE], refs[PLANE], refs[-1]
    for s in range(planes):
        plane = lax.rem(where[0] + s, planes)
        for t in range(PLANE):
            pltpu.make_async_copy(held[t].at[s], out.at[plane, t], sem).start()
    pltpu.make_async_copy(out, out, sem).wait()


def regroup(where, held):
    planes = held[0].shape[0]
    return pl.pallas_call(
        functools.partial(regroup_kernel, planes),
        out_shape=jax.ShapeDtypeStruct((planes, PLANE, *held[0].shape[1:]), held[0].dtype),
        in_specs=[SMEM, *[VMEM] * PLANE],
        out_specs=HBM,
        scratch_shapes=[pltpu.SemaphoreType.DMA],
        compiler_params=pltpu.CompilerParams(vmem_limit_bytes=VMEM_BYTES),
        cost_estimate=SMALL,
        name="regroup",
    )(where, *held)


def plane_pack_kernel(dims, cap, first, where, lists, last_lists, panels, last_panels, *rest):
    groups, planes, adapters, stride, last_stride, own = dims
    outs, sems = rest[:-1], rest[-1]
    share = outs[0].shape[1]
    mine = pl.ds(pl.multiple_of(first + where[1] * share, share), share)
    for i, out in enumerate(outs):
        plane = lax.rem(where[0] + i + 1, planes)

        def send(k, carry, out=out, plane=plane, i=i):
            pltpu.make_async_copy(panels.at[lists[plane * stride + k], mine], out.at[k], sems.at[i]).start()
            return carry

        def send_last(k, carry, out=out, plane=plane, i=i):
            adapter = last_lists[plane * last_stride + k]
            pltpu.make_async_copy(last_panels.at[adapter, mine], out.at[cap + k], sems.at[i]).start()
            return carry

        lax.fori_loop(0, cap, send, 0)
        lax.fori_loop(0, out.shape[0] - cap, send_last, 0)
    for i, out in enumerate(outs):
        pltpu.make_async_copy(out, out, sems.at[i]).wait()


def plane_pack(dims, caps, first, ranks, where, lists, last_lists, panels, last_panels):
    groups, planes = dims[:2]
    out = jax.ShapeDtypeStruct((sum(caps), ranks // groups, panels.shape[2]), panels.dtype)
    return pl.pallas_call(
        functools.partial(plane_pack_kernel, dims, caps[0], first),
        out_shape=(out,) * (planes - 1),
        in_specs=[SMEM, SMEM, SMEM, VMEM, VMEM],
        out_specs=(HBM,) * (planes - 1),
        scratch_shapes=[pltpu.SemaphoreType.DMA((planes - 1,))],
        compiler_params=pltpu.CompilerParams(vmem_limit_bytes=VMEM_BYTES),
        cost_estimate=SMALL,
        name="plane_pack",
    )(where, lists, last_lists, panels, last_panels)


def group_pack_kernel(dims, cap, where, places, last_places, *rest):
    groups, planes, adapters, stride, last_stride, own = dims
    got, outs, sems = rest[: planes - 1], rest[planes - 1 : -1], rest[-1]
    blocks = PLANE * own
    for i, out in enumerate(outs):
        group = lax.rem(where[1] + i + 1, groups)

        def send(j, place, out=out, i=i):
            for s in range(planes - 1):
                pltpu.make_async_copy(got[s].at[place], out.at[j, s], sems.at[i]).start()

        def send_block(j, carry, send=send, group=group):
            send(j, places[group * blocks + j])
            return carry

        lax.fori_loop(0, blocks, send_block, 0)
        for shard in range(PLANE):
            send(blocks + shard, cap + last_places[group * PLANE + shard])
    for i, out in enumerate(outs):
        pltpu.make_async_copy(out, out, sems.at[i]).wait()


def group_pack(dims, cap, where, places, last_places, got):
    groups, planes, adapters, stride, last_stride, own = dims
    out = jax.ShapeDtypeStruct((PLANE * (own + 1), planes - 1, *got[0].shape[1:]), got[0].dtype)
    return pl.pallas_call(
        functools.partial(group_pack_kernel, dims, cap),
        out_shape=(out,) * (groups - 1),
        in_specs=[SMEM, SMEM, SMEM, *[VMEM] * (planes - 1)],
        out_specs=(HBM,) * (groups - 1),
        scratch_shapes=[pltpu.SemaphoreType.DMA((groups - 1,))],
        compiler_params=pltpu.CompilerParams(vmem_limit_bytes=VMEM_BYTES),
        cost_estimate=SMALL,
        name="group_pack",
    )(where, places, last_places, *got)


def shard_pack_kernel(dims, cap, first, where, places, last_places, ids, panels, last_panels, *rest):
    groups, planes, adapters, stride, last_stride, own = dims
    got = rest[: planes - 1]
    swapped = rest[planes - 1 : planes + groups - 2]
    outs, sems = rest[planes + groups - 2 : -1], rest[-1]
    ranks, share = outs[0].shape[2], got[0].shape[1]
    my_group, my_shard = where[1], where[2]

    def part(group):
        return pl.ds(pl.multiple_of(group * share, share), share)

    for t, out in enumerate(outs):
        shard = lax.rem(my_shard + t, PLANE)

        def send(b, source, place, behind, out=out, t=t):
            copy = lambda src, dst: pltpu.make_async_copy(src, dst, sems.at[t]).start()
            copy(source.at[pl.ds(first, ranks)], out.at[b, 0])
            for s in range(planes - 1):
                copy(got[s].at[place], out.at[b, s + 1, part(my_group)])
            for d in range(groups - 1):
                other = lax.rem(my_group + groups - d - 1, groups)
                copy(swapped[d].at[behind], out.at[b, pl.ds(1, planes - 1), part(other)])

        def send_block(b, carry, send=send, shard=shard):
            j = shard * own + b
            send(b, panels.at[ids[j]], places[my_group * PLANE * own + j], j)
            return carry

        lax.fori_loop(0, own, send_block, 0)
        last = last_panels.at[ids[shard * own + own - 1]]
        send(own, last, cap + last_places[my_group * PLANE + shard], PLANE * own + shard)
    for t, out in enumerate(outs):
        pltpu.make_async_copy(out, out, sems.at[t]).wait()


def shard_pack(dims, cap, first, ranks, where, places, last_places, ids, panels, last_panels, got, swapped):
    groups, planes, adapters, stride, last_stride, own = dims
    out = jax.ShapeDtypeStruct((own + 1, planes, ranks, panels.shape[2]), panels.dtype)
    return pl.pallas_call(
        functools.partial(shard_pack_kernel, dims, cap, first),
        out_shape=(out,) * PLANE,
        in_specs=[*[SMEM] * 4, VMEM, VMEM, *[VMEM] * (planes + groups - 2)],
        out_specs=(HBM,) * PLANE,
        scratch_shapes=[pltpu.SemaphoreType.DMA((PLANE,))],
        compiler_params=pltpu.CompilerParams(vmem_limit_bytes=VMEM_BYTES),
        cost_estimate=SMALL,
        name="shard_pack",
    )(where, places, last_places, ids, panels, last_panels, *got, *swapped)


def shrink_kernel(planes, where, tokens, *rest):
    maps, out = rest[:-1], rest[-1]
    width = maps[0].shape[-1]
    total = jnp.zeros(out.shape, jnp.float32)
    for t in range(PLANE):
        shard = lax.rem(where[2] + PLANE - t, PLANE)
        for s in range(planes):
            source = lax.rem(where[0] + planes - s, planes) * PLANE + shard
            total += lax.dot_general(
                tokens[:, pl.ds(pl.multiple_of(source * width, width), width)],
                jnp.concatenate([m[0, s] for m in maps[t::PLANE]], axis=0),
                (((1,), (1,)), ((), ())),
                preferred_element_type=jnp.float32,
            )
    out[...] = total.astype(out.dtype)


def shrink(where, tokens, maps):
    own, (planes, ranks, width) = tokens.shape[0] // BLOCK, maps[0].shape[1:]
    rank = len(maps) // PLANE * ranks
    return pl.pallas_call(
        functools.partial(shrink_kernel, planes),
        grid=(own,),
        out_shape=jax.ShapeDtypeStruct((own * BLOCK, rank), tokens.dtype),
        in_specs=[
            SMEM,
            pl.BlockSpec((BLOCK, tokens.shape[1]), lambda b: (b, 0)),
            *[pl.BlockSpec((1, planes, ranks, width), lambda b: (b, 0, 0, 0))] * len(maps),
        ],
        out_specs=pl.BlockSpec((BLOCK, rank), lambda b: (b, 0)),
        compiler_params=pltpu.CompilerParams(vmem_limit_bytes=VMEM_BYTES),
        cost_estimate=SMALL,
        name="shrink",
    )(where, tokens, *maps)


def expand_kernel(where, ids, count, scales, shrunk, direct, *rest):
    last, out = rest[:-1], rest[-1]
    b = pl.program_id(0)
    scale = scales[ids[b]]
    planes, width = direct.shape[0], direct.shape[-1]
    rows = b * BLOCK + lax.broadcasted_iota(jnp.int32, (BLOCK, width), 0)
    live = rows < count[0]

    def write(plane, t, panel):
        source = plane * PLANE + lax.rem(where[2] + PLANE - t, PLANE)
        part = jnp.dot(shrunk[...], panel, preferred_element_type=jnp.float32)
        columns = pl.ds(pl.multiple_of(source * width, width), width)
        out[:, columns] = jnp.where(live, part * scale, 0.0).astype(out.dtype)

    @pl.when(b < pl.num_programs(0) - 1)
    def _():
        for plane in range(planes):
            for t in range(PLANE):
                write(plane, t, direct[plane, t, 0])

    @pl.when(b == pl.num_programs(0) - 1)
    def _():
        for s in range(planes):
            for t in range(PLANE):
                panel = jnp.concatenate([m[0, s] for m in last[t::PLANE]], axis=0)
                write(lax.rem(where[0] + planes - s, planes), t, panel)


def expand(where, ids, count, scales, shrunk, direct, maps):
    planes, _, blocks, rank, width = direct.shape
    own, ranks = blocks + 1, maps[0].shape[2]
    columns = planes * PLANE * width
    return pl.pallas_call(
        expand_kernel,
        grid=(own,),
        out_shape=jax.ShapeDtypeStruct((own * BLOCK, columns), shrunk.dtype),
        in_specs=[
            *[SMEM] * 4,
            pl.BlockSpec((BLOCK, rank), lambda b: (b, 0)),
            pl.BlockSpec((planes, PLANE, 1, rank, width), lambda b: (0, 0, jnp.minimum(b, blocks - 1), 0, 0)),
            *[pl.BlockSpec((1, planes, ranks, width), lambda b: (own, 0, 0, 0))] * len(maps),
        ],
        out_specs=pl.BlockSpec((BLOCK, columns), lambda b: (b, 0)),
        compiler_params=pltpu.CompilerParams(vmem_limit_bytes=VMEM_BYTES),
        cost_estimate=SMALL,
        name="expand",
    )(where, ids, count, scales, shrunk, direct, *maps)


def body(groups, tokens, shrink_panels, expand_panels, adapter_scale, block_adapter, shard_counts):
    devices = shard_counts.shape[0]
    own = tokens.shape[0] // BLOCK
    planes = devices // PLANE
    adapters = shrink_panels.shape[0]
    most = min(adapters, groups * PLANE * own)
    last_most = min(adapters, groups * PLANE)
    dims = (groups, planes, adapters, most + 1, last_most + 1, own)
    caps = tuple((most * part // 32, last_most * last // 8) for part, last in CAPS)

    ids = block_adapter.reshape(-1)
    me, group = lax.axis_index("blk"), lax.axis_index("groups")
    where = jnp.stack([me // PLANE, group, lax.rem(me, PLANE)]).astype(jnp.int32)
    facts = jnp.concatenate([ids, shard_counts])
    known = [facts]
    for d in range(1, groups):
        known.append(lax.ppermute(facts, "groups", [(i, (i + d) % groups) for i in range(groups)]))
    *up_sent, lists, last_lists, places, last_places, pick = prepare(dims, caps, where, known, expand_panels)
    plane_ids = lax.dynamic_slice_in_dim(ids, me // PLANE * PLANE * own, PLANE * own, 0)
    mine = lax.dynamic_slice_in_dim(ids, me * own, own, 0)
    count = lax.dynamic_slice_in_dim(shard_counts, me, 1, 0)
    down_panels = jnp.swapaxes(shrink_panels, 1, 2)

    def plane_shift(x, s):
        return lax.ppermute(x, "blk", [(i, (i + s * PLANE) % devices) for i in range(devices)])

    def group_shift(x, d):
        return lax.ppermute(x, "groups", [(i, (i + d) % groups) for i in range(groups)])

    def shard_shift(x, t):
        pairs = [(i, i // PLANE * PLANE + (i + t) % PLANE) for i in range(devices)]
        return lax.ppermute(x, "blk", pairs)

    rank = expand_panels.shape[1]
    parts = 2 if rank % (2 * groups * ROWS) == 0 else 1
    ranks = rank // parts
    panels = (down_panels, expand_panels)

    def run(caps):
        def branch(up_sent):
            sent = [
                plane_pack(dims, caps, h * ranks, ranks, where, lists, last_lists, *panels) for h in range(parts)
            ]
            near = [up_sent[0], *[shard_shift(up_sent[t], t) for t in range(1, PLANE)]]
            up_packed = regroup(where, near)
            got, maps = [], []
            for h in range(parts):
                got.append([plane_shift(x, s + 1) for s, x in enumerate(sent[h])])
                if h + 1 < parts:
                    got[h], sent[h + 1] = lax.optimization_barrier((got[h], sent[h + 1]))
                else:
                    got[h], maps, up_packed = lax.optimization_barrier((got[h], maps, up_packed))
                swaps = group_pack(dims, caps[0], where, places, last_places, got[h])
                swapped = [group_shift(x, d + 1) for d, x in enumerate(swaps)]
                maps.append(
                    shard_pack(
                        dims, caps[0], h * ranks, ranks, where, places, last_places, plane_ids, *panels, got[h], swapped
                    )
                )
            mirrors = [list(range(i, devices, PLANE)) for i in range(PLANE)]
            up = lax.all_to_all(up_packed, "blk", split_axis=0, concat_axis=0, tiled=True, axis_index_groups=mirrors)
            routed = []
            for kept, *moved in maps:
                routed += [kept, *[shard_shift(x, t + 1) for t, x in enumerate(moved)]]
            shrunk = shrink(where, tokens, routed)
            return expand(where, mine, count, adapter_scale, shrunk, up, routed)

        return branch

    return lax.switch(pick[0], [run(pair) for pair in caps], up_sent)


def solution(mesh):
    return jax.shard_map(
        functools.partial(body, mesh.shape["groups"]),
        mesh=mesh,
        in_specs=(
            P(("groups", "blk"), None),
            P(None, "blk", None),
            P(None, None, "blk"),
            P(),
            P("groups", None),
            P("groups"),
        ),
        out_specs=P(("groups", "blk"), None),
        check_vma=False,
    )
```

```python
import functools

import jax
import jax.numpy as jnp
from jax import lax
from jax.experimental import pallas as pl
from jax.experimental.pallas import tpu as pltpu
from jax.sharding import PartitionSpec as P

BLOCK = 64
ROWS = 16
CAPS = (16, 17, 18, 19, 20, 21, 22, 24, 28, 40)
PLANE = 4
VMEM_BYTES = 60 * 2**20

SMEM = pl.BlockSpec(memory_space=pltpu.SMEM)
VMEM = pl.BlockSpec(memory_space=pltpu.VMEM)
HBM = pl.BlockSpec(memory_space=pl.ANY)


SMALL = pl.CostEstimate(flops=0, bytes_accessed=1024, transcendentals=0)


def prepare_kernel(dims, caps, where, *rest):
    groups, planes, adapters, stride, own = dims
    facts, panels = rest[:groups], rest[groups]
    sent, rest = rest[groups + 1 : groups + 1 + PLANE], rest[groups + 1 + PLANE :]
    lists, bounds, places, last_places, pick, slot, last_slot, last_list, known, sems = rest
    plane_blocks = PLANE * own
    blocks = planes * plane_blocks
    row = blocks + planes * PLANE
    my_plane, my_group, my_shard = where[0], where[1], where[2]

    for t, out in enumerate(sent):
        shard = lax.rem(my_shard + t, PLANE)

        def send(s, carry, out=out, shard=shard, t=t):
            base = (lax.rem(my_plane + s, planes) * PLANE + shard) * own
            for b in range(own - 1):
                pltpu.make_async_copy(panels.at[facts[0][base + b]], out.at[s, b], sems.at[t]).start()
            return carry

        lax.fori_loop(0, planes, send, 0)

    for d, fact in enumerate(facts):
        base = lax.rem(my_group - d + groups, groups) * row

        def keep(i, carry, fact=fact, base=base):
            for k in range(PLANE):
                known[base + i * PLANE + k] = fact[i * PLANE + k]
            return carry

        lax.fori_loop(0, row // PLANE, keep, 0)

    def one_plane(plane, largest):
        at_slot, at_list = plane * adapters, plane * stride

        def clear(i, carry):
            for k in range(8):
                slot[at_slot + i * 8 + k] = -1
                last_slot[at_slot + i * 8 + k] = -1
            return carry

        lax.fori_loop(0, adapters // 8, clear, 0)
        found, last_found = jnp.int32(0), jnp.int32(0)
        for group in range(groups):
            for shard in range(PLANE):
                count = known[group * row + blocks + plane * PLANE + shard]
                for k in range(own):
                    adapter = known[group * row + plane * plane_blocks + shard * own + k]
                    held = slot[at_slot + adapter]
                    new = jnp.logical_and(count > k * BLOCK, held < 0)
                    slot[at_slot + adapter] = jnp.where(new, found, held)
                    lists[at_list + found] = adapter
                    found = found + new.astype(jnp.int32)
                held = last_slot[at_slot + adapter]
                new = jnp.logical_and(count > (own - 1) * BLOCK, held < 0)
                last_slot[at_slot + adapter] = jnp.where(new, last_found, held)
                last_list[last_found] = adapter
                last_found = last_found + new.astype(jnp.int32)

        def append(i, carry):
            lists[at_list + found + i] = last_list[i]
            return carry

        def fill(i, carry):
            lists[at_list + i] = 0
            return carry

        bounds[plane] = found
        lax.fori_loop(0, last_found, append, 0)
        lax.fori_loop(found + last_found, stride, fill, 0)
        return jnp.maximum(largest, found + last_found)

    largest = lax.fori_loop(0, planes, one_plane, jnp.int32(0))
    branch = jnp.int32(0)
    for cap in caps[:-1]:
        branch = branch + (largest > cap).astype(jnp.int32)
    pick[0] = branch

    def one_group(group, carry):
        for block in range(plane_blocks):
            adapter = known[group * row + my_plane * plane_blocks + block]
            places[group * plane_blocks + block] = jnp.maximum(slot[my_plane * adapters + adapter], 0)
            if block % own == own - 1:
                place = bounds[my_plane] + last_slot[my_plane * adapters + adapter]
                last_places[group * PLANE + block // own] = jnp.maximum(place, 0)
        return carry

    lax.fori_loop(0, groups, one_group, 0)
    for t, out in enumerate(sent):
        pltpu.make_async_copy(out, out, sems.at[t]).wait()


def prepare(dims, caps, where, facts, panels):
    groups, planes, adapters, stride, own = dims
    ints = lambda n: jax.ShapeDtypeStruct((n,), jnp.int32)
    sent = jax.ShapeDtypeStruct((planes, own - 1, *panels.shape[1:]), panels.dtype)
    row = planes * PLANE * (own + 1)
    counts = (planes * stride, planes, groups * PLANE * own, groups * PLANE, 1)
    return pl.pallas_call(
        functools.partial(prepare_kernel, dims, caps),
        out_shape=(*(sent,) * PLANE, *map(ints, counts)),
        in_specs=[SMEM, *[SMEM] * groups, VMEM],
        out_specs=(*(HBM,) * PLANE, *(SMEM,) * len(counts)),
        scratch_shapes=[
            pltpu.SMEM((planes * adapters,), jnp.int32),
            pltpu.SMEM((planes * adapters,), jnp.int32),
            pltpu.SMEM((groups * PLANE + 1,), jnp.int32),
            pltpu.SMEM((groups * row,), jnp.int32),
            pltpu.SemaphoreType.DMA((PLANE,)),
        ],
        compiler_params=pltpu.CompilerParams(vmem_limit_bytes=VMEM_BYTES),
        cost_estimate=SMALL,
        name="prepare",
    )(where, *facts, panels)


def regroup_kernel(planes, where, *refs):
    held, out, sem = refs[:PLANE], refs[PLANE], refs[-1]
    for s in range(planes):
        plane = lax.rem(where[0] + s, planes)
        for t in range(PLANE):
            pltpu.make_async_copy(held[t].at[s], out.at[plane, t], sem).start()
    pltpu.make_async_copy(out, out, sem).wait()


def regroup(where, held):
    planes = held[0].shape[0]
    return pl.pallas_call(
        functools.partial(regroup_kernel, planes),
        out_shape=jax.ShapeDtypeStruct((planes, PLANE, *held[0].shape[1:]), held[0].dtype),
        in_specs=[SMEM, *[VMEM] * PLANE],
        out_specs=HBM,
        scratch_shapes=[pltpu.SemaphoreType.DMA],
        compiler_params=pltpu.CompilerParams(vmem_limit_bytes=VMEM_BYTES),
        cost_estimate=SMALL,
        name="regroup",
    )(where, *held)


def plane_pack_kernel(dims, first, where, lists, bounds, panels, last_panels, *rest):
    groups, planes, adapters, stride, own = dims
    outs, (held, last_held, held_sems, sems) = rest[:-4], rest[-4:]
    share = outs[0].shape[1]
    mine = pl.ds(pl.multiple_of(first + where[1] * share, share), share)
    loads = [
        pltpu.make_async_copy(panels.at[:, mine], held, held_sems.at[0]),
        pltpu.make_async_copy(last_panels.at[:, mine], last_held, held_sems.at[1]),
    ]
    for load in loads:
        load.start()
    for load in loads:
        load.wait()
    for i, out in enumerate(outs):
        plane = lax.rem(where[0] + i + 1, planes)

        def send(k, carry, out=out, plane=plane, i=i):
            pltpu.make_async_copy(held.at[lists[plane * stride + k]], out.at[k], sems.at[i]).start()
            return carry

        def send_last(k, carry, out=out, plane=plane, i=i):
            pltpu.make_async_copy(last_held.at[lists[plane * stride + k]], out.at[k], sems.at[i]).start()
            return carry

        lax.fori_loop(0, bounds[plane], send, 0)
        lax.fori_loop(bounds[plane], out.shape[0], send_last, 0)
    for i, out in enumerate(outs):
        pltpu.make_async_copy(out, out, sems.at[i]).wait()


def plane_pack(dims, cap, first, ranks, where, lists, bounds, panels, last_panels):
    groups, planes = dims[:2]
    out = jax.ShapeDtypeStruct((cap, ranks // groups, panels.shape[2]), panels.dtype)
    return pl.pallas_call(
        functools.partial(plane_pack_kernel, dims, first),
        out_shape=(out,) * (planes - 1),
        in_specs=[SMEM, SMEM, SMEM, HBM, HBM],
        out_specs=(HBM,) * (planes - 1),
        scratch_shapes=[
            pltpu.VMEM((panels.shape[0], *out.shape[1:]), panels.dtype),
            pltpu.VMEM((panels.shape[0], *out.shape[1:]), panels.dtype),
            pltpu.SemaphoreType.DMA((2,)),
            pltpu.SemaphoreType.DMA((planes - 1,)),
        ],
        compiler_params=pltpu.CompilerParams(vmem_limit_bytes=VMEM_BYTES),
        cost_estimate=SMALL,
        name="plane_pack",
    )(where, lists, bounds, panels, last_panels)


def group_pack_kernel(dims, where, places, last_places, *rest):
    groups, planes, adapters, stride, own = dims
    got, outs, sems = rest[: planes - 1], rest[planes - 1 : -1], rest[-1]
    blocks = PLANE * own
    for i, out in enumerate(outs):
        group = lax.rem(where[1] + i + 1, groups)

        def send(j, place, out=out, i=i):
            for s in range(planes - 1):
                pltpu.make_async_copy(got[s].at[place], out.at[j, s], sems.at[i]).start()

        def send_block(j, carry, send=send, group=group):
            send(j, places[group * blocks + j])
            return carry

        lax.fori_loop(0, blocks, send_block, 0)
        for shard in range(PLANE):
            send(blocks + shard, last_places[group * PLANE + shard])
    for i, out in enumerate(outs):
        pltpu.make_async_copy(out, out, sems.at[i]).wait()


def group_pack(dims, where, places, last_places, got):
    groups, planes, adapters, stride, own = dims
    out = jax.ShapeDtypeStruct((PLANE * (own + 1), planes - 1, *got[0].shape[1:]), got[0].dtype)
    return pl.pallas_call(
        functools.partial(group_pack_kernel, dims),
        out_shape=(out,) * (groups - 1),
        in_specs=[SMEM, SMEM, SMEM, *[VMEM] * (planes - 1)],
        out_specs=(HBM,) * (groups - 1),
        scratch_shapes=[pltpu.SemaphoreType.DMA((groups - 1,))],
        compiler_params=pltpu.CompilerParams(vmem_limit_bytes=VMEM_BYTES),
        cost_estimate=SMALL,
        name="group_pack",
    )(where, places, last_places, *got)


def shard_pack_kernel(dims, first, where, places, last_places, ids, panels, last_panels, *rest):
    groups, planes, adapters, stride, own = dims
    got = rest[: planes - 1]
    swapped = rest[planes - 1 : planes + groups - 2]
    outs, sems = rest[planes + groups - 2 : -1], rest[-1]
    ranks, share = outs[0].shape[2], got[0].shape[1]
    my_group, my_shard = where[1], where[2]

    def part(group):
        return pl.ds(pl.multiple_of(group * share, share), share)

    for t, out in enumerate(outs):
        shard = lax.rem(my_shard + t, PLANE)

        def send(b, source, place, behind, out=out, t=t):
            copy = lambda src, dst: pltpu.make_async_copy(src, dst, sems.at[t]).start()
            copy(source.at[pl.ds(first, ranks)], out.at[b, 0])
            for s in range(planes - 1):
                copy(got[s].at[place], out.at[b, s + 1, part(my_group)])
            for d in range(groups - 1):
                other = lax.rem(my_group + groups - d - 1, groups)
                copy(swapped[d].at[behind], out.at[b, pl.ds(1, planes - 1), part(other)])

        def send_block(b, carry, send=send, shard=shard):
            j = shard * own + b
            send(b, panels.at[ids[j]], places[my_group * PLANE * own + j], j)
            return carry

        lax.fori_loop(0, own, send_block, 0)
        last = last_panels.at[ids[shard * own + own - 1]]
        send(own, last, last_places[my_group * PLANE + shard], PLANE * own + shard)
    for t, out in enumerate(outs):
        pltpu.make_async_copy(out, out, sems.at[t]).wait()


def shard_pack(dims, first, ranks, where, places, last_places, ids, panels, last_panels, got, swapped):
    groups, planes, adapters, stride, own = dims
    out = jax.ShapeDtypeStruct((own + 1, planes, ranks, panels.shape[2]), panels.dtype)
    return pl.pallas_call(
        functools.partial(shard_pack_kernel, dims, first),
        out_shape=(out,) * PLANE,
        in_specs=[*[SMEM] * 4, VMEM, VMEM, *[VMEM] * (planes + groups - 2)],
        out_specs=(HBM,) * PLANE,
        scratch_shapes=[pltpu.SemaphoreType.DMA((PLANE,))],
        compiler_params=pltpu.CompilerParams(vmem_limit_bytes=VMEM_BYTES),
        cost_estimate=SMALL,
        name="shard_pack",
    )(where, places, last_places, ids, panels, last_panels, *got, *swapped)


def shrink_kernel(planes, where, tokens, *rest):
    maps, out = rest[:-1], rest[-1]
    width = maps[0].shape[-1]
    total = jnp.zeros(out.shape, jnp.float32)
    for t in range(PLANE):
        shard = lax.rem(where[2] + PLANE - t, PLANE)
        for s in range(planes):
            source = lax.rem(where[0] + planes - s, planes) * PLANE + shard
            total += lax.dot_general(
                tokens[:, pl.ds(pl.multiple_of(source * width, width), width)],
                jnp.concatenate([m[0, s] for m in maps[t::PLANE]], axis=0),
                (((1,), (1,)), ((), ())),
                preferred_element_type=jnp.float32,
            )
    out[...] = total.astype(out.dtype)


def shrink(where, tokens, maps):
    own, (planes, ranks, width) = tokens.shape[0] // BLOCK, maps[0].shape[1:]
    rank = len(maps) // PLANE * ranks
    return pl.pallas_call(
        functools.partial(shrink_kernel, planes),
        grid=(own,),
        out_shape=jax.ShapeDtypeStruct((own * BLOCK, rank), tokens.dtype),
        in_specs=[
            SMEM,
            pl.BlockSpec((BLOCK, tokens.shape[1]), lambda b: (b, 0)),
            *[pl.BlockSpec((1, planes, ranks, width), lambda b: (b, 0, 0, 0))] * len(maps),
        ],
        out_specs=pl.BlockSpec((BLOCK, rank), lambda b: (b, 0)),
        compiler_params=pltpu.CompilerParams(vmem_limit_bytes=VMEM_BYTES),
        cost_estimate=SMALL,
        name="shrink",
    )(where, tokens, *maps)


def expand_kernel(where, ids, count, scales, shrunk, direct, *rest):
    last, out = rest[:-1], rest[-1]
    b = pl.program_id(0)
    scale = scales[ids[b]]
    planes, width = direct.shape[0], direct.shape[-1]
    rows = b * BLOCK + lax.broadcasted_iota(jnp.int32, (BLOCK, width), 0)
    live = rows < count[0]

    def write(plane, t, panel):
        source = plane * PLANE + lax.rem(where[2] + PLANE - t, PLANE)
        part = jnp.dot(shrunk[...], panel, preferred_element_type=jnp.float32)
        columns = pl.ds(pl.multiple_of(source * width, width), width)
        out[:, columns] = jnp.where(live, part * scale, 0.0).astype(out.dtype)

    @pl.when(b < pl.num_programs(0) - 1)
    def _():
        for plane in range(planes):
            for t in range(PLANE):
                write(plane, t, direct[plane, t, 0])

    @pl.when(b == pl.num_programs(0) - 1)
    def _():
        for s in range(planes):
            for t in range(PLANE):
                panel = jnp.concatenate([m[0, s] for m in last[t::PLANE]], axis=0)
                write(lax.rem(where[0] + planes - s, planes), t, panel)


def expand(where, ids, count, scales, shrunk, direct, maps):
    planes, _, blocks, rank, width = direct.shape
    own, ranks = blocks + 1, maps[0].shape[2]
    columns = planes * PLANE * width
    return pl.pallas_call(
        expand_kernel,
        grid=(own,),
        out_shape=jax.ShapeDtypeStruct((own * BLOCK, columns), shrunk.dtype),
        in_specs=[
            *[SMEM] * 4,
            pl.BlockSpec((BLOCK, rank), lambda b: (b, 0)),
            pl.BlockSpec((planes, PLANE, 1, rank, width), lambda b: (0, 0, jnp.minimum(b, blocks - 1), 0, 0)),
            *[pl.BlockSpec((1, planes, ranks, width), lambda b: (own, 0, 0, 0))] * len(maps),
        ],
        out_specs=pl.BlockSpec((BLOCK, columns), lambda b: (b, 0)),
        compiler_params=pltpu.CompilerParams(vmem_limit_bytes=VMEM_BYTES),
        cost_estimate=SMALL,
        name="expand",
    )(where, ids, count, scales, shrunk, direct, *maps)


def body(groups, tokens, shrink_panels, expand_panels, adapter_scale, block_adapter, shard_counts):
    devices = shard_counts.shape[0]
    own = tokens.shape[0] // BLOCK
    planes = devices // PLANE
    adapters = shrink_panels.shape[0]
    most = min(adapters, groups * PLANE * own)
    last_most = min(adapters, groups * PLANE)
    most += last_most
    dims = (groups, planes, adapters, most + 1, own)
    caps = tuple(most * part // CAPS[-1] for part in CAPS)

    ids = block_adapter.reshape(-1)
    me, group = lax.axis_index("blk"), lax.axis_index("groups")
    where = jnp.stack([me // PLANE, group, lax.rem(me, PLANE)]).astype(jnp.int32)
    facts = jnp.concatenate([ids, shard_counts])
    known = [facts]
    for d in range(1, groups):
        known.append(lax.ppermute(facts, "groups", [(i, (i + d) % groups) for i in range(groups)]))
    *up_sent, lists, bounds, places, last_places, pick = prepare(dims, caps, where, known, expand_panels)
    plane_ids = lax.dynamic_slice_in_dim(ids, me // PLANE * PLANE * own, PLANE * own, 0)
    mine = lax.dynamic_slice_in_dim(ids, me * own, own, 0)
    count = lax.dynamic_slice_in_dim(shard_counts, me, 1, 0)
    down_panels = jnp.swapaxes(shrink_panels, 1, 2)

    def plane_shift(x, s):
        return lax.ppermute(x, "blk", [(i, (i + s * PLANE) % devices) for i in range(devices)])

    def group_shift(x, d):
        return lax.ppermute(x, "groups", [(i, (i + d) % groups) for i in range(groups)])

    def shard_shift(x, t):
        pairs = [(i, i // PLANE * PLANE + (i + t) % PLANE) for i in range(devices)]
        return lax.ppermute(x, "blk", pairs)

    rank = expand_panels.shape[1]
    parts = 2 if rank % (2 * groups * ROWS) == 0 else 1
    ranks = rank // parts
    panels = (down_panels, expand_panels)

    def run(cap):
        def branch(up_sent):
            sent = [
                plane_pack(dims, cap, h * ranks, ranks, where, lists, bounds, *panels) for h in range(parts)
            ]
            near = [up_sent[0], *[shard_shift(up_sent[t], t) for t in range(1, PLANE)]]
            up_packed = regroup(where, near)
            got, maps = [], []
            for h in range(parts):
                got.append([plane_shift(x, s + 1) for s, x in enumerate(sent[h])])
                if h + 1 < parts:
                    got[h], sent[h + 1] = lax.optimization_barrier((got[h], sent[h + 1]))
                else:
                    got[h], maps, up_packed = lax.optimization_barrier((got[h], maps, up_packed))
                swaps = group_pack(dims, where, places, last_places, got[h])
                swapped = [group_shift(x, d + 1) for d, x in enumerate(swaps)]
                maps.append(
                    shard_pack(
                        dims, h * ranks, ranks, where, places, last_places, plane_ids, *panels, got[h], swapped
                    )
                )
            mirrors = [list(range(i, devices, PLANE)) for i in range(PLANE)]
            up = lax.all_to_all(up_packed, "blk", split_axis=0, concat_axis=0, tiled=True, axis_index_groups=mirrors)
            routed = []
            for kept, *moved in maps:
                routed += [kept, *[shard_shift(x, t + 1) for t, x in enumerate(moved)]]
            shrunk = shrink(where, tokens, routed)
            return expand(where, mine, count, adapter_scale, shrunk, up, routed)

        return branch

    return lax.switch(pick[0], [run(cap) for cap in caps], up_sent)


def solution(mesh):
    return jax.shard_map(
        functools.partial(body, mesh.shape["groups"]),
        mesh=mesh,
        in_specs=(
            P(("groups", "blk"), None),
            P(None, "blk", None),
            P(None, None, "blk"),
            P(),
            P("groups", None),
            P("groups"),
        ),
        out_specs=P(("groups", "blk"), None),
        check_vma=False,
    )
```

```python
import functools

import jax
import jax.numpy as jnp
from jax import lax
from jax.experimental import pallas as pl
from jax.experimental.pallas import tpu as pltpu
from jax.sharding import PartitionSpec as P

BLOCK = 64
ROWS = 16
CAPS = (16, 17, 18, 19, 20, 21, 22, 24, 28, 40)
PLANE = 4
VMEM_BYTES = 60 * 2**20

SMEM = pl.BlockSpec(memory_space=pltpu.SMEM)
VMEM = pl.BlockSpec(memory_space=pltpu.VMEM)
HBM = pl.BlockSpec(memory_space=pl.ANY)


SMALL = pl.CostEstimate(flops=0, bytes_accessed=1024, transcendentals=0)


def prepare_kernel(dims, caps, where, *rest):
    groups, planes, adapters, stride, own = dims
    facts, panels = rest[:groups], rest[groups]
    sent, rest = rest[groups + 1 : groups + 1 + PLANE], rest[groups + 1 + PLANE :]
    lists, bounds, places, last_places, pick, slot, last_slot, last_list, known, sems = rest
    plane_blocks = PLANE * own
    blocks = planes * plane_blocks
    row = blocks + planes * PLANE
    my_plane, my_group, my_shard = where[0], where[1], where[2]

    for t, out in enumerate(sent):
        shard = lax.rem(my_shard + t, PLANE)

        def send(s, carry, out=out, shard=shard, t=t):
            base = (lax.rem(my_plane + s, planes) * PLANE + shard) * own
            for b in range(own - 1):
                pltpu.make_async_copy(panels.at[facts[0][base + b]], out.at[s, b], sems.at[t]).start()
            return carry

        lax.fori_loop(0, planes, send, 0)

    for d, fact in enumerate(facts):
        base = lax.rem(my_group - d + groups, groups) * row

        def keep(i, carry, fact=fact, base=base):
            for k in range(PLANE):
                known[base + i * PLANE + k] = fact[i * PLANE + k]
            return carry

        lax.fori_loop(0, row // PLANE, keep, 0)

    def one_plane(plane, largest):
        at_slot, at_list = plane * adapters, plane * stride

        def clear(i, carry):
            for k in range(8):
                slot[at_slot + i * 8 + k] = -1
                last_slot[at_slot + i * 8 + k] = -1
            return carry

        lax.fori_loop(0, adapters // 8, clear, 0)
        found, last_found = jnp.int32(0), jnp.int32(0)
        for group in range(groups):
            for shard in range(PLANE):
                count = known[group * row + blocks + plane * PLANE + shard]
                for k in range(own):
                    adapter = known[group * row + plane * plane_blocks + shard * own + k]
                    held = slot[at_slot + adapter]
                    new = jnp.logical_and(count > k * BLOCK, held < 0)
                    slot[at_slot + adapter] = jnp.where(new, found, held)
                    lists[at_list + found] = adapter
                    found = found + new.astype(jnp.int32)
                held = last_slot[at_slot + adapter]
                new = jnp.logical_and(count > (own - 1) * BLOCK, held < 0)
                last_slot[at_slot + adapter] = jnp.where(new, last_found, held)
                last_list[last_found] = adapter
                last_found = last_found + new.astype(jnp.int32)

        def append(i, carry):
            lists[at_list + found + i] = last_list[i]
            return carry

        def fill(i, carry):
            lists[at_list + i] = 0
            return carry

        bounds[plane] = found
        lax.fori_loop(0, last_found, append, 0)
        lax.fori_loop(found + last_found, stride, fill, 0)
        return jnp.maximum(largest, found + last_found)

    largest = lax.fori_loop(0, planes, one_plane, jnp.int32(0))
    branch = jnp.int32(0)
    for cap in caps[:-1]:
        branch = branch + (largest > cap).astype(jnp.int32)
    pick[0] = branch

    def one_group(group, carry):
        for block in range(plane_blocks):
            adapter = known[group * row + my_plane * plane_blocks + block]
            places[group * plane_blocks + block] = jnp.maximum(slot[my_plane * adapters + adapter], 0)
            if block % own == own - 1:
                place = bounds[my_plane] + last_slot[my_plane * adapters + adapter]
                last_places[group * PLANE + block // own] = jnp.maximum(place, 0)
        return carry

    lax.fori_loop(0, groups, one_group, 0)
    for t, out in enumerate(sent):
        pltpu.make_async_copy(out, out, sems.at[t]).wait()


def prepare(dims, caps, where, facts, panels):
    groups, planes, adapters, stride, own = dims
    ints = lambda n: jax.ShapeDtypeStruct((n,), jnp.int32)
    sent = jax.ShapeDtypeStruct((planes, own - 1, *panels.shape[1:]), panels.dtype)
    row = planes * PLANE * (own + 1)
    counts = (planes * stride, planes, groups * PLANE * own, groups * PLANE, 1)
    return pl.pallas_call(
        functools.partial(prepare_kernel, dims, caps),
        out_shape=(*(sent,) * PLANE, *map(ints, counts)),
        in_specs=[SMEM, *[SMEM] * groups, VMEM],
        out_specs=(*(HBM,) * PLANE, *(SMEM,) * len(counts)),
        scratch_shapes=[
            pltpu.SMEM((planes * adapters,), jnp.int32),
            pltpu.SMEM((planes * adapters,), jnp.int32),
            pltpu.SMEM((groups * PLANE + 1,), jnp.int32),
            pltpu.SMEM((groups * row,), jnp.int32),
            pltpu.SemaphoreType.DMA((PLANE,)),
        ],
        compiler_params=pltpu.CompilerParams(vmem_limit_bytes=VMEM_BYTES),
        cost_estimate=SMALL,
        name="prepare",
    )(where, *facts, panels)


def regroup_kernel(planes, where, *refs):
    held, out, sem = refs[:PLANE], refs[PLANE], refs[-1]
    for s in range(planes):
        plane = lax.rem(where[0] + s, planes)
        for t in range(PLANE):
            pltpu.make_async_copy(held[t].at[s], out.at[plane, t], sem).start()
    pltpu.make_async_copy(out, out, sem).wait()


def regroup(where, held):
    planes = held[0].shape[0]
    return pl.pallas_call(
        functools.partial(regroup_kernel, planes),
        out_shape=jax.ShapeDtypeStruct((planes, PLANE, *held[0].shape[1:]), held[0].dtype),
        in_specs=[SMEM, *[VMEM] * PLANE],
        out_specs=HBM,
        scratch_shapes=[pltpu.SemaphoreType.DMA],
        compiler_params=pltpu.CompilerParams(vmem_limit_bytes=VMEM_BYTES),
        cost_estimate=SMALL,
        name="regroup",
    )(where, *held)


def plane_pack_kernel(dims, first, where, lists, bounds, panels, last_panels, *rest):
    groups, planes, adapters, stride, own = dims
    outs, (held, last_held, held_sems, sems) = rest[:-4], rest[-4:]
    share = outs[0].shape[1]
    mine = pl.ds(pl.multiple_of(first + where[1] * share, share), share)
    loads = [
        pltpu.make_async_copy(panels.at[:, mine], held, held_sems.at[0]),
        pltpu.make_async_copy(last_panels.at[:, mine], last_held, held_sems.at[1]),
    ]
    for load in loads:
        load.start()
    for load in loads:
        load.wait()
    for i, out in enumerate(outs):
        plane = lax.rem(where[0] + i + 1, planes)

        def send(k, carry, out=out, plane=plane, i=i):
            pltpu.make_async_copy(held.at[lists[plane * stride + k]], out.at[k], sems.at[i]).start()
            return carry

        def send_last(k, carry, out=out, plane=plane, i=i):
            pltpu.make_async_copy(last_held.at[lists[plane * stride + k]], out.at[k], sems.at[i]).start()
            return carry

        lax.fori_loop(0, bounds[plane], send, 0)
        lax.fori_loop(bounds[plane], out.shape[0], send_last, 0)
    for i, out in enumerate(outs):
        pltpu.make_async_copy(out, out, sems.at[i]).wait()


def plane_pack(dims, cap, first, ranks, where, lists, bounds, panels, last_panels):
    groups, planes = dims[:2]
    out = jax.ShapeDtypeStruct((cap, ranks // groups, panels.shape[2]), panels.dtype)
    return pl.pallas_call(
        functools.partial(plane_pack_kernel, dims, first),
        out_shape=(out,) * (planes - 1),
        in_specs=[SMEM, SMEM, SMEM, HBM, HBM],
        out_specs=(HBM,) * (planes - 1),
        scratch_shapes=[
            pltpu.VMEM((panels.shape[0], *out.shape[1:]), panels.dtype),
            pltpu.VMEM((panels.shape[0], *out.shape[1:]), panels.dtype),
            pltpu.SemaphoreType.DMA((2,)),
            pltpu.SemaphoreType.DMA((planes - 1,)),
        ],
        compiler_params=pltpu.CompilerParams(vmem_limit_bytes=VMEM_BYTES),
        cost_estimate=SMALL,
        name="plane_pack",
    )(where, lists, bounds, panels, last_panels)


def group_pack_kernel(dims, where, places, last_places, *rest):
    groups, planes, adapters, stride, own = dims
    got, outs, sems = rest[: planes - 1], rest[planes - 1 : -1], rest[-1]
    blocks = PLANE * own
    for i, out in enumerate(outs):
        group = lax.rem(where[1] + i + 1, groups)

        def send(j, place, out=out, i=i):
            for s in range(planes - 1):
                pltpu.make_async_copy(got[s].at[place], out.at[j, s], sems.at[i]).start()

        def send_block(j, carry, send=send, group=group):
            send(j, places[group * blocks + j])
            return carry

        lax.fori_loop(0, blocks, send_block, 0)
        for shard in range(PLANE):
            send(blocks + shard, last_places[group * PLANE + shard])
    for i, out in enumerate(outs):
        pltpu.make_async_copy(out, out, sems.at[i]).wait()


def group_pack(dims, where, places, last_places, got):
    groups, planes, adapters, stride, own = dims
    out = jax.ShapeDtypeStruct((PLANE * (own + 1), planes - 1, *got[0].shape[1:]), got[0].dtype)
    return pl.pallas_call(
        functools.partial(group_pack_kernel, dims),
        out_shape=(out,) * (groups - 1),
        in_specs=[SMEM, SMEM, SMEM, *[VMEM] * (planes - 1)],
        out_specs=(HBM,) * (groups - 1),
        scratch_shapes=[pltpu.SemaphoreType.DMA((groups - 1,))],
        compiler_params=pltpu.CompilerParams(vmem_limit_bytes=VMEM_BYTES),
        cost_estimate=SMALL,
        name="group_pack",
    )(where, places, last_places, *got)


def shard_pack_kernel(dims, first, where, places, last_places, ids, panels, last_panels, *rest):
    groups, planes, adapters, stride, own = dims
    got = rest[: planes - 1]
    swapped = rest[planes - 1 : planes + groups - 2]
    outs, sems = rest[planes + groups - 2 : -1], rest[-1]
    ranks, share = outs[0].shape[2], got[0].shape[1]
    my_group, my_shard = where[1], where[2]

    def part(group):
        return pl.ds(pl.multiple_of(group * share, share), share)

    for t, out in enumerate(outs):
        shard = lax.rem(my_shard + t, PLANE)

        def send(b, source, place, behind, out=out, t=t):
            copy = lambda src, dst: pltpu.make_async_copy(src, dst, sems.at[t]).start()
            copy(source.at[pl.ds(first, ranks)], out.at[b, 0])
            for s in range(planes - 1):
                copy(got[s].at[place], out.at[b, s + 1, part(my_group)])
            for d in range(groups - 1):
                other = lax.rem(my_group + groups - d - 1, groups)
                copy(swapped[d].at[behind], out.at[b, pl.ds(1, planes - 1), part(other)])

        def send_block(b, carry, send=send, shard=shard):
            j = shard * own + b
            send(b, panels.at[ids[j]], places[my_group * PLANE * own + j], j)
            return carry

        lax.fori_loop(0, own, send_block, 0)
        last = last_panels.at[ids[shard * own + own - 1]]
        send(own, last, last_places[my_group * PLANE + shard], PLANE * own + shard)
    for t, out in enumerate(outs):
        pltpu.make_async_copy(out, out, sems.at[t]).wait()


def shard_pack(dims, first, ranks, where, places, last_places, ids, panels, last_panels, got, swapped):
    groups, planes, adapters, stride, own = dims
    out = jax.ShapeDtypeStruct((own + 1, planes, ranks, panels.shape[2]), panels.dtype)
    return pl.pallas_call(
        functools.partial(shard_pack_kernel, dims, first),
        out_shape=(out,) * PLANE,
        in_specs=[*[SMEM] * 4, VMEM, VMEM, *[VMEM] * (planes + groups - 2)],
        out_specs=(HBM,) * PLANE,
        scratch_shapes=[pltpu.SemaphoreType.DMA((PLANE,))],
        compiler_params=pltpu.CompilerParams(vmem_limit_bytes=VMEM_BYTES),
        cost_estimate=SMALL,
        name="shard_pack",
    )(where, places, last_places, ids, panels, last_panels, *got, *swapped)


def shrink_kernel(planes, where, tokens, *rest):
    maps, out = rest[:-1], rest[-1]
    width = maps[0].shape[-1]
    total = jnp.zeros(out.shape, jnp.float32)
    for t in range(PLANE):
        shard = lax.rem(where[2] + PLANE - t, PLANE)
        for s in range(planes):
            source = lax.rem(where[0] + planes - s, planes) * PLANE + shard
            total += lax.dot_general(
                tokens[:, pl.ds(pl.multiple_of(source * width, width), width)],
                jnp.concatenate([m[0, s] for m in maps[t::PLANE]], axis=0),
                (((1,), (1,)), ((), ())),
                preferred_element_type=jnp.float32,
            )
    out[...] = total.astype(out.dtype)


def shrink(where, tokens, maps):
    own, (planes, ranks, width) = tokens.shape[0] // BLOCK, maps[0].shape[1:]
    rank = len(maps) // PLANE * ranks
    return pl.pallas_call(
        functools.partial(shrink_kernel, planes),
        grid=(own,),
        out_shape=jax.ShapeDtypeStruct((own * BLOCK, rank), tokens.dtype),
        in_specs=[
            SMEM,
            pl.BlockSpec((BLOCK, tokens.shape[1]), lambda b: (b, 0)),
            *[pl.BlockSpec((1, planes, ranks, width), lambda b: (b, 0, 0, 0))] * len(maps),
        ],
        out_specs=pl.BlockSpec((BLOCK, rank), lambda b: (b, 0)),
        compiler_params=pltpu.CompilerParams(vmem_limit_bytes=VMEM_BYTES // 2),
        cost_estimate=SMALL,
        name="shrink",
    )(where, tokens, *maps)


def expand_kernel(where, ids, count, scales, shrunk, direct, *rest):
    last, out = rest[:-1], rest[-1]
    b = pl.program_id(0)
    scale = scales[ids[b]]
    planes, width = direct.shape[0], direct.shape[-1]
    rows = b * BLOCK + lax.broadcasted_iota(jnp.int32, (BLOCK, width), 0)
    live = rows < count[0]

    def write(plane, t, panel):
        source = plane * PLANE + lax.rem(where[2] + PLANE - t, PLANE)
        part = jnp.dot(shrunk[...], panel, preferred_element_type=jnp.float32)
        columns = pl.ds(pl.multiple_of(source * width, width), width)
        out[:, columns] = jnp.where(live, part * scale, 0.0).astype(out.dtype)

    @pl.when(b < pl.num_programs(0) - 1)
    def _():
        for plane in range(planes):
            for t in range(PLANE):
                write(plane, t, direct[plane, t, 0])

    @pl.when(b == pl.num_programs(0) - 1)
    def _():
        for s in range(planes):
            for t in range(PLANE):
                panel = jnp.concatenate([m[0, s] for m in last[t::PLANE]], axis=0)
                write(lax.rem(where[0] + planes - s, planes), t, panel)


def expand(where, ids, count, scales, shrunk, direct, maps):
    planes, _, blocks, rank, width = direct.shape
    own, ranks = blocks + 1, maps[0].shape[2]
    columns = planes * PLANE * width
    return pl.pallas_call(
        expand_kernel,
        grid=(own,),
        out_shape=jax.ShapeDtypeStruct((own * BLOCK, columns), shrunk.dtype),
        in_specs=[
            *[SMEM] * 4,
            pl.BlockSpec((BLOCK, rank), lambda b: (b, 0)),
            pl.BlockSpec((planes, PLANE, 1, rank, width), lambda b: (0, 0, jnp.minimum(b, blocks - 1), 0, 0)),
            *[pl.BlockSpec((1, planes, ranks, width), lambda b: (own, 0, 0, 0))] * len(maps),
        ],
        out_specs=pl.BlockSpec((BLOCK, columns), lambda b: (b, 0)),
        compiler_params=pltpu.CompilerParams(vmem_limit_bytes=VMEM_BYTES),
        cost_estimate=SMALL,
        name="expand",
    )(where, ids, count, scales, shrunk, direct, *maps)


def body(groups, tokens, shrink_panels, expand_panels, adapter_scale, block_adapter, shard_counts):
    devices = shard_counts.shape[0]
    own = tokens.shape[0] // BLOCK
    planes = devices // PLANE
    adapters = shrink_panels.shape[0]
    most = min(adapters, groups * PLANE * own)
    last_most = min(adapters, groups * PLANE)
    most += last_most
    dims = (groups, planes, adapters, most + 1, own)
    caps = tuple(most * part // CAPS[-1] for part in CAPS)

    ids = block_adapter.reshape(-1)
    me, group = lax.axis_index("blk"), lax.axis_index("groups")
    where = jnp.stack([me // PLANE, group, lax.rem(me, PLANE)]).astype(jnp.int32)
    facts = jnp.concatenate([ids, shard_counts])
    known = [facts]
    for d in range(1, groups):
        known.append(lax.ppermute(facts, "groups", [(i, (i + d) % groups) for i in range(groups)]))
    *up_sent, lists, bounds, places, last_places, pick = prepare(dims, caps, where, known, expand_panels)
    plane_ids = lax.dynamic_slice_in_dim(ids, me // PLANE * PLANE * own, PLANE * own, 0)
    mine = lax.dynamic_slice_in_dim(ids, me * own, own, 0)
    count = lax.dynamic_slice_in_dim(shard_counts, me, 1, 0)
    down_panels = jnp.swapaxes(shrink_panels, 1, 2)

    def plane_shift(x, s):
        return lax.ppermute(x, "blk", [(i, (i + s * PLANE) % devices) for i in range(devices)])

    def group_shift(x, d):
        return lax.ppermute(x, "groups", [(i, (i + d) % groups) for i in range(groups)])

    def shard_shift(x, t):
        pairs = [(i, i // PLANE * PLANE + (i + t) % PLANE) for i in range(devices)]
        return lax.ppermute(x, "blk", pairs)

    rank = expand_panels.shape[1]
    parts = 2 if rank % (2 * groups * ROWS) == 0 else 1
    ranks = rank // parts
    panels = (down_panels, expand_panels)

    def run(cap):
        def branch(up_sent):
            sent = [
                plane_pack(dims, cap, h * ranks, ranks, where, lists, bounds, *panels) for h in range(parts)
            ]
            near = [up_sent[0], *[shard_shift(up_sent[t], t) for t in range(1, PLANE)]]
            up_packed = regroup(where, near)
            got, maps = [], []
            for h in range(parts):
                got.append([plane_shift(x, s + 1) for s, x in enumerate(sent[h])])
                if h + 1 < parts:
                    got[h], sent[h + 1] = lax.optimization_barrier((got[h], sent[h + 1]))
                else:
                    got[h], maps, up_packed = lax.optimization_barrier((got[h], maps, up_packed))
                swaps = group_pack(dims, where, places, last_places, got[h])
                swapped = [group_shift(x, d + 1) for d, x in enumerate(swaps)]
                maps.append(
                    shard_pack(
                        dims, h * ranks, ranks, where, places, last_places, plane_ids, *panels, got[h], swapped
                    )
                )
            mirrors = [list(range(i, devices, PLANE)) for i in range(PLANE)]
            up = lax.all_to_all(up_packed, "blk", split_axis=0, concat_axis=0, tiled=True, axis_index_groups=mirrors)
            routed = []
            for kept, *moved in maps:
                routed += [kept, *[shard_shift(x, t + 1) for t, x in enumerate(moved)]]
            shrunk = shrink(where, tokens, routed)
            return expand(where, mine, count, adapter_scale, shrunk, up, routed)

        return branch

    return lax.switch(pick[0], [run(cap) for cap in caps], up_sent)


def solution(mesh):
    return jax.shard_map(
        functools.partial(body, mesh.shape["groups"]),
        mesh=mesh,
        in_specs=(
            P(("groups", "blk"), None),
            P(None, "blk", None),
            P(None, None, "blk"),
            P(),
            P("groups", None),
            P("groups"),
        ),
        out_specs=P(("groups", "blk"), None),
        check_vma=False,
    )
```
